32 devices in a mesh: groups: 2 (over x), src: 8 (over z, y), tile: 2 (over core).
Axes of the slice: x: 2, y: 2, z: 4, core: 2. Of those that a mesh axis runs over, the one named last changes fastest.
Arguments:
- mask: float32 [2048, 1024], P(('groups', 'tile')), parts along dimension 0, may hold values from 0 to 1
- target: float32 [2048, 1024], P(('groups', 'tile')), parts along dimension 0, may hold values from 0 to 1
- pupil: float32 [64, 64], replicated, may hold values from 0.1 to 1.9
- source_shift: int32 [24, 2], replicated, may hold values from -24 to 24
- source_weight: float32 [24], replicated, may hold values from 0.25 to 4
Outputs:
- mask_gradient: float32 [2048, 1024], P(('groups', 'tile'), 'src'), parts along dimension 0
The draws below stay inside these ranges and needn't reach their ends.
There are 2 independent parts, one for each index of `groups`. The reference program is written for one: setup_inputs(seed, part) draws one part's arguments, and reference() takes and returns one part's arrays. A program takes and returns all parts, laid end to end along the dimension named above; an argument that names none is the same for every part. Nothing has to cross between parts.
Inputs may be any that keep to these rules, and one draw needn't show every extreme that they name: `source_shift`: integer frequency shifts of the source points.
All inputs are finite; a program needn't handle non-finite values.
Results may differ from the reference program's by a relative error of at most 0.0003.
Values sent between devices are 32-bit elements; how exact they have to be, the bound alone decides.
No kernel may reach another device: no remote copies, remote signals or barrier semaphores. Data moves between devices by JAX's collectives and lax.ppermute only.
A program may use at most 128 MiB of HBM per device.

```python
import math
import jax
import jax.numpy as jnp
from jax import lax

TS = 512
HALO = 64
K = 64
SRC_DEV = 3
GC = 2
PAD = 640
SOURCES = 24
ROWS = 1024
COLS = 1024
N_SRC = 8
N_TILE = 2


def place_ends(array, key, smallest, high):
    extent = array.shape
    index_at = [jax.random.randint(jax.random.fold_in(key, axis), (), 0, extent[axis]) for axis in range(len(extent))]
    array = array.at[tuple(index_at)].set(smallest)
    longest = extent.index(max(extent))
    index_at[longest] = (index_at[longest] + 1) % extent[longest]
    return array.at[tuple(index_at)].set(high)


def steps_of(own_key, extent, shards, low, largest):
    loudness = 1.0
    for axis_at, blocks in shards:
        draws = jax.random.uniform(jax.random.fold_in(jax.random.fold_in(own_key, 6), axis_at), (blocks,), jnp.float32, low / len(shards), largest / len(shards))
        loudness = loudness * jnp.repeat(jnp.exp(draws), extent[axis_at] // blocks).reshape((-1,) + (1,) * (len(extent) - 1 - axis_at))
    return loudness


def setup_inputs(seed: int = 0, part: int = 0) -> dict:
    splits = jax.random.split(jax.random.key(seed), 6)
    part_keys = jax.random.split(jax.random.fold_in(splits[5], part), 6)
    mask = jnp.clip(1.0 * jax.random.uniform(part_keys[0], (ROWS, COLS), jnp.float32) ** steps_of(part_keys[0], (ROWS, COLS), ((0, 2),), -0.2, 0.2), 0.0, 1.0)
    target = jnp.clip(1.0 * jax.random.uniform(part_keys[1], (ROWS, COLS), jnp.float32) ** steps_of(part_keys[1], (ROWS, COLS), ((0, 2),), -0.2, 0.2), 0.0, 1.0)
    pupil = jnp.clip(1.0 + 0.18 * jax.random.normal(splits[2], (K, K), jnp.float32), 0.1, 1.9)
    source_shift = place_ends(jax.random.randint(splits[3], (SOURCES, 2), -((3 * K) // 8), (3 * K) // 8 + 1), jax.random.fold_in(splits[3], 1), -((3 * K) // 8), ((3 * K) // 8 + 1) - 1).astype(jnp.int32)
    source_weight = jnp.clip(jnp.exp(jax.random.uniform(splits[4], (SOURCES,), jnp.float32, math.log(0.25), math.log(4.0))), 0.25, 4.0)
    return dict(mask=mask, target=target, pupil=pupil, source_shift=source_shift, source_weight=source_weight)


full_turn = 2.0 * math.pi
exact_mode = lax.Precision.HIGHEST
resist_gain = 25.0
resist_level = 0.25

def light_block(tiles, shift_block, weight_block, pupil):
    sources = shift_block.shape[0]
    freqs = pupil.shape[0]
    padded = tiles.shape[1]
    count = tiles.shape[0]
    scaling = full_turn / padded
    centred = jnp.arange(freqs, dtype=jnp.int32) - freqs // 2
    pixels = jnp.arange(padded, dtype=jnp.int32)
    row_freq = centred[None, :] + shift_block[:, 0:1]
    col_freq = centred[None, :] + shift_block[:, 1:2]
    row_phase = jnp.mod(row_freq[:, :, None] * pixels[None, None, :], padded).astype(jnp.float32) * scaling
    col_phase = jnp.mod(col_freq[:, :, None] * pixels[None, None, :], padded).astype(jnp.float32) * scaling
    col_table = jnp.concatenate([jnp.cos(col_phase), -jnp.sin(col_phase)], axis=1)
    col_table = col_table.reshape(sources * 2 * freqs, padded).T
    halfway = jnp.einsum('gxy,yn->gxn', tiles, col_table, precision=exact_mode)
    halfway = halfway.reshape(count, padded, sources, 2 * freqs)
    row_table = jnp.concatenate([jnp.cos(row_phase), jnp.sin(row_phase)], axis=1)
    products = jnp.einsum('sux,gxsn->gsun', row_table, halfway, precision=exact_mode)
    spec_real = (products[:, :, :freqs, :freqs] + products[:, :, freqs:, freqs:]) * pupil
    spec_imag = (products[:, :, :freqs, freqs:] - products[:, :, freqs:, :freqs]) * pupil
    outputs = jnp.arange(TS, dtype=jnp.int32) + HALO
    out_phase = jnp.mod(outputs[:, None] * centred[None, :], padded).astype(jnp.float32) * scaling
    back_cos = jnp.cos(out_phase) / padded
    back_sin = jnp.sin(out_phase) / padded
    back_stack = jnp.concatenate([back_cos, back_sin], axis=0)
    spectra = jnp.concatenate([spec_real, spec_imag], axis=-1)
    mixed = jnp.einsum('xu,gsun->gsxn', back_stack, spectra, precision=exact_mode)
    left_real = mixed[:, :, :TS, :freqs] - mixed[:, :, TS:, freqs:]
    left_imag = mixed[:, :, :TS, freqs:] + mixed[:, :, TS:, :freqs]
    rows_both = jnp.concatenate([left_real, left_imag], axis=-1)
    upper_half = jnp.concatenate([back_cos.T, back_sin.T], axis=1)
    lower_half = jnp.concatenate([-back_sin.T, back_cos.T], axis=1)
    right_table = jnp.concatenate([upper_half, lower_half], axis=0)
    field = jnp.einsum('gsxk,kn->gsxn', rows_both, right_table, precision=exact_mode)
    power = field[..., :TS] * field[..., :TS] + field[..., TS:] * field[..., TS:]
    return lax.optimization_barrier(jnp.sum(power * weight_block[None, :, None, None], axis=1))

def resist_slope(intensity, target):
    printed = jax.nn.sigmoid(resist_gain * (intensity - resist_level))
    return 2.0 * (printed - target) * resist_gain * printed * (1.0 - printed)

def tile_stack(mask_image):
    widened = jnp.pad(mask_image, HALO)
    pieces = []
    for tile_row in range(N_TILE):
        for tile_column in range(GC):
            pieces.append(widened[tile_row * TS:tile_row * TS + PAD, tile_column * TS:tile_column * TS + PAD])
    return jnp.stack(pieces)

def to_image(tiles):
    return tiles.reshape(N_TILE, GC, TS, TS).transpose(0, 2, 1, 3).reshape(N_TILE * TS, GC * TS)

def from_image(image):
    return image.reshape(N_TILE, TS, GC, TS).transpose(0, 2, 1, 3).reshape(N_TILE * GC, TS, TS)

def reference(mask, target, pupil, source_shift, source_weight):
    tiles, unstack = jax.vjp(tile_stack, mask)
    shift_blocks = source_shift.reshape(N_SRC, SRC_DEV, 2)
    weight_blocks = source_weight.reshape(N_SRC, SRC_DEV)
    total_weight = jnp.sum(source_weight)

    def forward_step(carry, block):
        return (carry + light_block(tiles, block[0], block[1], pupil), None)
    start = jnp.zeros((N_TILE * GC, TS, TS), jnp.float32)
    summed, _ = lax.scan(forward_step, start, (shift_blocks, weight_blocks))
    intensity = to_image(summed) / total_weight
    slope_tiles = from_image(resist_slope(intensity, target) / total_weight)

    def backward_step(carry, block):

        def local_light(tile_input):
            return light_block(tile_input, block[0], block[1], pupil)
        _, pullback = jax.vjp(local_light, tiles)
        return (carry + pullback(slope_tiles)[0], None)
    gathered, _ = lax.scan(backward_step, jnp.zeros_like(tiles), (shift_blocks, weight_blocks))
    return unstack(gathered)[0]
```

```python
import functools
import math

import jax
import jax.numpy as jnp
import ml_dtypes
import numpy as np
from jax import lax
from jax.experimental import pallas as pl
from jax.experimental.pallas import tpu as pltpu
from jax.sharding import PartitionSpec as P

TS = 512
HALO = 64
PAD = TS + 2 * HALO
LANES = 128

resist_gain = 25.0
resist_level = 0.25

f32 = jnp.float32
bf16 = jnp.bfloat16


def halves(table):
    table = np.asarray(table, np.float64)
    high = table.astype(np.float32).astype(ml_dtypes.bfloat16)
    low = (table - high.astype(np.float64)).astype(np.float32).astype(ml_dtypes.bfloat16)
    return high, low


def turns(left, right, period):
    angle = 2.0 * np.pi * np.mod(np.outer(left, right), period) / period
    return np.cos(angle), np.sin(angle)


def both(table, axis):
    return np.concatenate(halves(table), axis=axis)


def split(value):
    high = value.astype(bf16)
    return high, (value - high.astype(f32)).astype(bf16)


def dot(left, right):
    return lax.dot_general(left, right, (((1,), (0,)), ((), ())), preferred_element_type=f32)


class Plan:
    def __init__(self, freqs, rows, cols, n_src, n_tile):
        self.freqs = freqs
        self.reach = (3 * freqs) // 8
        self.band = 2 * freqs
        self.used = freqs + 2 * self.reach
        self.coarse = 2 * freqs
        self.tile_cols = cols // TS
        self.owners = n_src // self.tile_cols
        self.width = cols // n_src
        self.wide = -(-self.width // LANES) * LANES
        self.rim = min(self.width, HALO)
        self.hop = max(1, HALO // self.width)
        sides = min(2, self.tile_cols - 1)
        self.window = TS + sides * LANES
        self.window_start = [
            min(max(0, c * TS - LANES), cols - self.window) for c in range(self.tile_cols)
        ]
        self.cols = cols
        self.partner = {}
        for c in range(1, self.tile_cols):
            first = c * self.owners
            for k in range(self.hop):
                left, right = first - self.hop + k, first + k
                self.partner[left] = right
                self.partner[right] = left
        self.n_src = n_src
        self.n_tile = n_tile

    def tables(self):
        band, used, coarse = self.band, self.used, self.coarse
        index = np.arange(band)
        valid = (index < used).astype(np.float64)
        centre = index - (self.freqs // 2 + self.reach)
        pixels = np.arange(PAD)
        cosine, sine = turns(centre, pixels, PAD)
        rows = np.concatenate([cosine * valid[:, None], -sine * valid[:, None]], axis=0)
        out = {}
        own = rows[:, HALO : HALO + TS]
        out["e_own"] = both(own, 0)
        rims = [rows[:, HALO + TS :], rows[:, :HALO]]
        out["e_rim"] = np.stack([both(rim, 0) for rim in rims])
        col_tables = []
        for c in range(self.tile_cols):
            place = np.arange(self.window) + self.window_start[c] - c * TS + HALO
            inside = ((place >= 0) & (place < PAD)).astype(np.float64)
            cosine, sine = turns(place, centre, PAD)
            table = np.concatenate([cosine * valid, sine * valid], axis=1) * inside[:, None]
            col_tables.append(both(table, 1))
        out["col"] = np.stack(col_tables)
        freq = np.arange(self.freqs) - self.freqs // 2
        points = np.arange(coarse)
        cosine, sine = turns(points, freq, coarse)
        high, low = halves(np.concatenate([cosine, -sine], axis=1))
        out["up_rows"] = np.concatenate(
            [np.concatenate([high, high], axis=1), np.concatenate([low, low], axis=1)], axis=0
        )
        to_field = np.concatenate(
            [np.concatenate([cosine.T, sine.T], axis=1), np.concatenate([-sine.T, cosine.T], axis=1)],
            axis=0,
        )
        high, low = halves(to_field)
        stacked = np.concatenate([high, low], axis=1)
        out["up_cols"] = np.concatenate([stacked, stacked], axis=0)
        out["down_cols"] = both(to_field.T, 1)
        high, low = halves(np.concatenate([cosine.T, sine.T], axis=0))
        out["down_rows"] = np.concatenate(
            [np.concatenate([high, high], axis=1), np.concatenate([low, low], axis=1)], axis=0
        )
        spread = (np.arange(TS) + HALO)[:, None] - (PAD // coarse) * points[None, :]
        harmonics = np.arange(1, self.freqs)
        weave = np.ones(spread.shape)
        for p in harmonics:
            weave = weave + 2.0 * np.cos(2.0 * np.pi * np.mod(p * spread, PAD) / PAD)
        weave = weave / coarse
        out["weave"] = both(weave, 1)
        turned = both(weave.T, 1)
        out["weave_up"] = np.concatenate([turned, turned], axis=0)
        out["weave_down"] = both(weave.T, 0)
        blocks = []
        for j in range(self.n_src):
            c = j // self.owners
            pieces = []
            for target, span in ((j, self.width), (self.partner.get(j), self.rim)):
                cosine = np.zeros((band, self.wide))
                sine = np.zeros((band, self.wide))
                if target is not None:
                    first = target * self.width
                    if target != j and target < j:
                        first += self.width - span
                    place = np.arange(first, first + span) - c * TS + HALO
                    cosine[:, :span], sine[:, :span] = turns(centre, place, PAD)
                cosine, sine = cosine * valid[:, None], sine * valid[:, None]
                pieces.append((cosine, sine))
            upper = np.concatenate([t for cosine, sine in pieces for t in (cosine, sine)], axis=1)
            lower = np.concatenate([t for cosine, sine in pieces for t in (-sine, cosine)], axis=1)
            blocks.append(both(np.concatenate([upper, lower], axis=0), 1))
        out["final_cols"] = np.stack(blocks)
        out["final_rows"] = np.stack(halves(rows.T))
        return {name: np.ascontiguousarray(value) for name, value in out.items()}


TABLES = (
    "e_own", "e_rim", "col", "up_rows", "up_cols", "down_cols", "down_rows",
    "weave", "weave_up", "weave_down", "final_cols", "final_rows",
)


def image_kernel(plan, *refs):
    (shift, weight, pupil, mask, target, halo, *rest) = refs
    tabs = dict(zip(TABLES, rest[: len(TABLES)]))
    rest = rest[len(TABLES) :]
    own_out, row_out, col_out, corner_out = rest[:4]
    (
        mask_v, target_v, e_rim, col_tab, final_tab, spectrum, fields, grads, whole_grad, u_high, u_low, woven, sems,
    ) = rest[4:]
    sources = shift.shape[0]
    freqs, reach, band, coarse = plan.freqs, plan.reach, plan.band, plan.coarse
    tile_row = lax.axis_index("tile")
    block = lax.axis_index("src")
    tile_col = block // plan.owners
    start = tile_col * 0
    for c in range(plan.tile_cols):
        start = jnp.where(tile_col == c, plan.window_start[c] // LANES, start)
    start = pl.multiple_of(start * LANES, LANES)
    copies = [
        pltpu.make_async_copy(mask.at[:, pl.ds(start, plan.window)], mask_v, sems.at[0]),
        pltpu.make_async_copy(tabs["e_rim"].at[tile_row], e_rim, sems.at[1]),
        pltpu.make_async_copy(tabs["col"].at[tile_col], col_tab, sems.at[2]),
        pltpu.make_async_copy(
            target.at[:, pl.ds(pl.multiple_of(tile_col * TS, TS), TS)], target_v, sems.at[3]
        ),
        pltpu.make_async_copy(tabs["final_cols"].at[block], final_tab, sems.at[4]),
    ]
    for copy in copies:
        copy.start()
    total = weight[0]
    for s in range(1, sources):
        total = total + weight[s]
    pupils = pupil[...]
    pupils = jnp.concatenate([pupils, pupils], axis=1)
    lane = lax.broadcasted_iota(jnp.int32, (freqs, band), 1)
    first_half = lane < freqs

    copies[0].wait()
    copies[1].wait()
    e_own, rim_table = tabs["e_own"], e_rim[...]
    for n in range(0, plan.window, 256):
        span = min(256, plan.window - n)
        high, low = split(mask_v[:, n : n + span])
        rim_high, rim_low = split(halo[:, n : n + span])
        part = dot(e_own[...], high) + dot(rim_table, rim_high)
        rows = part[: 2 * band] + part[2 * band :]
        rows = rows + dot(e_own[: 2 * band, :], low) + dot(rim_table[: 2 * band], rim_low)
        high, low = split(rows)
        u_high[:, n : n + span] = high
        u_low[:, n : n + span] = low
    copies[2].wait()
    prod = dot(u_high[...], col_tab[...])
    prod = prod[:, : 2 * band] + prod[:, 2 * band :] + dot(u_low[...], col_tab[:, : 2 * band])
    scale = 1.0 / (PAD * PAD)
    spectrum[0] = (prod[:band, :band] + prod[band:, band:]) * scale
    spectrum[1] = (prod[band:, :band] - prod[:band, band:]) * scale

    def window_of(s):
        down = shift[s, 0] + reach
        along = shift[s, 1] + reach
        real = spectrum[0, pl.ds(down, freqs), :]
        imag = spectrum[1, pl.ds(down, freqs), :]
        near, far = lax.rem(band - along, band), lax.rem(band + freqs - along, band)
        upper = jnp.where(first_half, pltpu.roll(real, near, 1), pltpu.roll(imag, far, 1))
        lower = jnp.where(first_half, pltpu.roll(imag, near, 1), -pltpu.roll(real, far, 1))
        return jnp.concatenate([upper * pupils, lower * pupils], axis=0)

    def forward(i, power):
        both_windows = jnp.concatenate([window_of(2 * i), window_of(2 * i + 1)], axis=1)
        high, low = split(both_windows)
        lifted = dot(tabs["up_rows"][...], jnp.concatenate([high, low], axis=0))
        lifted = lifted[:coarse] + lifted[coarse:]
        high, low = split(lifted)
        for k in range(2):
            s = 2 * i + k
            left = jnp.concatenate([high[:, k * band : (k + 1) * band], low[:, k * band : (k + 1) * band]], axis=1)
            field = dot(left, tabs["up_cols"][...])
            field = field[:, : 2 * coarse] + field[:, 2 * coarse :]
            fields[s] = field
            square = field * field
            power = power + (weight[s] / total) * (square[:, :coarse] + square[:, coarse:])
        return power

    power = lax.fori_loop(0, sources // 2, forward, jnp.zeros((coarse, coarse), f32))

    copies[3].wait()
    high, low = split(power)
    power_pair = jnp.concatenate([high, low], axis=1)
    power_quad = jnp.concatenate([power_pair, power_pair], axis=0)
    chunk = 128
    for m in range(0, TS, chunk):
        left = dot(tabs["weave"][m : m + chunk, :], power_quad)
        high, low = split(left[:, :coarse] + left[:, coarse:])
        light = dot(jnp.concatenate([high, low], axis=1), tabs["weave_up"][...])
        light = light[:, :TS] + light[:, TS:]
        printed = 1.0 / (1.0 + jnp.exp(-resist_gain * (light - resist_level)))
        slope = (2.0 * resist_gain) * (printed - target_v[m : m + chunk, :]) * printed * (1.0 - printed)
        high, low = split(slope)
        part = dot(high, tabs["weave"][...]) + dot(low, tabs["weave"][...])
        high, low = split(part[:, :coarse] + part[:, coarse:])
        woven[m : m + chunk, :] = jnp.concatenate([high, low], axis=1)
    part = dot(tabs["weave_down"][...], woven[...])
    part = part[:coarse] + part[coarse:]
    pull = part[:, :coarse] + part[:, coarse:]
    pull = jnp.concatenate([pull, pull], axis=1)

    grads[...] = jnp.zeros_like(grads)
    sign = jnp.where(first_half, 1.0, -1.0).astype(f32)

    def backward(i, carry):
        pieces = []
        for k in range(2):
            s = 2 * i + k
            push = fields[s] * (pull * (2.0 * weight[s] / total))
            high, low = split(push)
            part = dot(high, tabs["down_cols"][...]) + dot(low, tabs["down_cols"][...])
            pieces.append(part[:, :band] + part[:, band:])
        high, low = split(jnp.concatenate(pieces, axis=1))
        part = dot(tabs["down_rows"][...], jnp.concatenate([high, low], axis=0))
        part = part[:band] + part[band:]
        for k in range(2):
            s = 2 * i + k
            mine = part[:, k * band : (k + 1) * band]
            mine = (mine[:freqs] + sign * pltpu.roll(mine[freqs:], freqs, 1)) * pupils
            down = shift[s, 0] + reach
            along = shift[s, 1] + reach
            near, far = along, lax.rem(band + along - freqs, band)
            zero = jnp.zeros_like(mine)
            grads[0, pl.ds(down, freqs), :] += pltpu.roll(jnp.where(first_half, mine, zero), near, 1)
            grads[1, pl.ds(down, freqs), :] += pltpu.roll(jnp.where(first_half, zero, mine), far, 1)
        return carry

    lax.fori_loop(0, sources // 2, backward, 0)

    copies[4].wait()
    wide = plan.wide
    bands = jnp.concatenate([grads[0], grads[1]], axis=1) * scale
    high, low = split(bands)
    part = dot(high, final_tab[...])
    part = part[:, : 4 * wide] + part[:, 4 * wide :] + dot(low, final_tab[:, : 4 * wide])
    part = jnp.concatenate(
        [
            jnp.concatenate([part[:, :wide], part[:, 2 * wide : 3 * wide]], axis=1),
            jnp.concatenate([part[:, wide : 2 * wide], part[:, 3 * wide :]], axis=1),
        ],
        axis=0,
    )
    high, low = split(part)
    rows_high, rows_low = tabs["final_rows"][0], tabs["final_rows"][1]
    whole_grad[...] = dot(rows_high, high) + dot(rows_high, low) + dot(rows_low, high)
    own_out[...] = whole_grad[HALO : HALO + TS, : plan.width]
    col_out[...] = whole_grad[HALO : HALO + TS, wide : wide + plan.rim]
    rim_start = pl.multiple_of(jnp.where(tile_row == 0, HALO + TS, 0), HALO)
    row_out[...] = whole_grad[pl.ds(rim_start, HALO), : plan.width]
    corner_out[...] = whole_grad[pl.ds(rim_start, HALO), wide : wide + plan.rim]


def finish_kernel(plan, own, row, col, corner, out):
    tile_row = lax.axis_index("tile")
    block = lax.axis_index("src")
    tile_col = block // plan.owners
    copies = plan.width // plan.rim
    on_left = block - tile_col * plan.owners >= plan.owners // 2
    slot = jnp.where(on_left, copies - 1, 0)

    def placed(piece):
        value = piece[...]
        if copies == 1:
            return value
        value = jnp.concatenate([value] * copies, axis=1)
        lane = lax.broadcasted_iota(jnp.int32, value.shape, 1)
        return jnp.where(lane // plan.rim == slot, value, jnp.zeros_like(value))

    out[...] = own[...] + placed(col)
    first = pl.multiple_of(jnp.where(tile_row == 0, TS - HALO, 0), HALO)
    out[pl.ds(first, HALO), :] += row[...] + placed(corner)


def shards(plan, mask, target, pupil, source_shift, source_weight):
    tile_row = lax.axis_index("tile")
    block = lax.axis_index("src")
    tile_col = block // plan.owners
    starts = jnp.asarray(plan.window_start, jnp.int32)
    swap = [(0, 1), (1, 0)]
    edge = lax.dynamic_slice(
        mask, (jnp.where(tile_row == 0, TS - HALO, 0), starts[tile_col]), (HALO, plan.window)
    )
    halo = lax.ppermute(edge, "tile", swap)
    tables = plan.tables()
    vmem = pl.BlockSpec(memory_space=pltpu.VMEM)
    smem = pl.BlockSpec(memory_space=pltpu.SMEM)
    anywhere = pl.BlockSpec(memory_space=pl.ANY)
    far = ("e_rim", "col", "final_cols")
    sources = source_shift.shape[0]
    band, coarse = plan.band, plan.coarse
    parts = pl.pallas_call(
        functools.partial(image_kernel, plan),
        out_shape=[
            jax.ShapeDtypeStruct((TS, plan.width), f32),
            jax.ShapeDtypeStruct((HALO, plan.width), f32),
            jax.ShapeDtypeStruct((TS, plan.rim), f32),
            jax.ShapeDtypeStruct((HALO, plan.rim), f32),
        ],
        in_specs=[smem, smem, vmem, anywhere, anywhere, vmem]
        + [anywhere if name in far else vmem for name in TABLES],
        out_specs=[vmem] * 4,
        scratch_shapes=[
            pltpu.VMEM((TS, plan.window), f32),
            pltpu.VMEM((TS, TS), f32),
            pltpu.VMEM(tables["e_rim"].shape[1:], bf16),
            pltpu.VMEM(tables["col"].shape[1:], bf16),
            pltpu.VMEM(tables["final_cols"].shape[1:], bf16),
            pltpu.VMEM((2, band, band), f32),
            pltpu.VMEM((sources, coarse, 2 * coarse), f32),
            pltpu.VMEM((2, band, band), f32),
            pltpu.VMEM((PAD, 2 * plan.wide), f32),
            pltpu.VMEM((2 * band, plan.window), bf16),
            pltpu.VMEM((2 * band, plan.window), bf16),
            pltpu.VMEM((TS, 2 * coarse), bf16),
            pltpu.SemaphoreType.DMA((5,)),
        ],
        compiler_params=pltpu.CompilerParams(vmem_limit_bytes=56 * 1024 * 1024),
        name="image",
    )(source_shift, source_weight, pupil, mask, target, halo, *[jnp.asarray(tables[name]) for name in TABLES])
    own, row, col, corner = parts
    row = lax.ppermute(row, "tile", swap)
    pairs = sorted(plan.partner.items())
    col = lax.ppermute(col, "src", pairs)
    crossing = [
        (left * plan.n_tile + t, right * plan.n_tile + 1 - t) for left, right in pairs for t in range(2)
    ]
    corner = lax.ppermute(corner, ("src", "tile"), crossing)
    return pl.pallas_call(
        functools.partial(finish_kernel, plan),
        out_shape=jax.ShapeDtypeStruct((TS, plan.width), f32),
        in_specs=[vmem] * 4,
        out_specs=vmem,
        name="finish",
    )(own, row, col, corner)


def solution(mesh):
    sizes = dict(mesh.shape)

    def run(mask, target, pupil, source_shift, source_weight):
        local_rows = mask.shape[0] // (sizes["groups"] * sizes["tile"])
        plan = Plan(pupil.shape[0], local_rows, mask.shape[1], sizes["src"], sizes["tile"])
        placed = (P(("groups", "tile"), None), P(("groups", "tile"), None), P(), P(), P())
        return jax.shard_map(
            functools.partial(shards, plan),
            mesh=mesh,
            in_specs=placed,
            out_specs=P(("groups", "tile"), "src"),
            check_vma=False,
        )(mask, target, pupil, source_shift, source_weight)

    return run
```

```python
import functools
import math

import jax
import jax.numpy as jnp
import ml_dtypes
import numpy as np
from jax import lax
from jax.experimental import pallas as pl
from jax.experimental.pallas import tpu as pltpu
from jax.sharding import PartitionSpec as P

TS = 512
HALO = 64
PAD = TS + 2 * HALO
LANES = 128
SKEW = 12
FINE = 512
MOST = 24

resist_gain = 25.0
resist_level = 0.25

f32 = jnp.float32
bf16 = jnp.bfloat16


def halves(table):
    table = np.asarray(table, np.float64)
    high = table.astype(np.float32).astype(ml_dtypes.bfloat16)
    low = (table - high.astype(np.float64)).astype(np.float32).astype(ml_dtypes.bfloat16)
    return high, low


def turns(left, right, period):
    angle = 2.0 * np.pi * np.mod(np.outer(left, right), period) / period
    return np.cos(angle), np.sin(angle)


def both(table, axis):
    return np.concatenate(halves(table), axis=axis)


def split(value):
    high = value.astype(bf16)
    return high, (value - high.astype(f32)).astype(bf16)


def dot(left, right):
    return lax.dot_general(left, right, (((1,), (0,)), ((), ())), preferred_element_type=f32)


class Plan:
    def __init__(self, freqs, cols, n_src, sources):
        self.freqs = freqs
        self.reach = (3 * freqs) // 8
        self.band = 2 * freqs
        self.coarse = 2 * freqs
        self.cols = cols
        self.tile_cols = cols // TS
        self.width = cols // n_src
        self.wide = -(-self.width // LANES) * LANES
        self.n_src = n_src
        self.sources = sources
        self.group = max(n for n in range(2, MOST + 1, 2) if sources % n == 0)
        self.stores = self.tile_cols if sources <= MOST else 1
        self.spans = [
            (max(0, c * TS - LANES), min(cols, (c + 1) * TS + LANES)) for c in range(self.tile_cols)
        ]

    def tables(self):
        freqs, band, coarse = self.freqs, self.band, self.coarse
        index = np.arange(band)
        used = (index < freqs + 2 * self.reach).astype(np.float64)
        centre = index - (freqs // 2 + self.reach)
        out = {}
        cosine, sine = turns(centre, np.arange(PAD), PAD)
        rows = np.concatenate([cosine, -sine], axis=0) * np.concatenate([used, used])[:, None]
        out["e_own"] = both(rows[:, HALO : HALO + TS], 0)
        out["e_rim"] = np.stack([both(rows[:, HALO + TS :], 0), both(rows[:, :HALO], 0)])
        out["final_rows"] = np.stack(halves(rows.T))

        def fold(real, imag):
            return np.concatenate(
                [real[:, :freqs], imag[:, :freqs], real[:, freqs:], imag[:, freqs:]], axis=1
            )

        for c, (first, last) in enumerate(self.spans):
            place = np.arange(first, last) - c * TS + HALO
            inside = ((place >= 0) & (place < PAD)).astype(np.float64)[:, None] * used
            cosine, sine = turns(place, centre, PAD)
            cosine, sine = cosine * inside, sine * inside
            out[f"col{c}"] = both(np.concatenate([fold(cosine, -sine), fold(sine, cosine)], axis=0), 1)
        relative = np.arange(freqs) - freqs // 2
        points = np.arange(coarse)
        cosine, sine = turns(points, relative, coarse)
        high, low = halves(np.concatenate([cosine, -sine], axis=1))
        out["up_rows"] = np.concatenate(
            [np.concatenate([high, high], axis=1), np.concatenate([low, low], axis=1)], axis=0
        )
        high, low = halves(np.concatenate([cosine.T, sine.T], axis=0))
        out["down_rows"] = np.concatenate(
            [np.concatenate([high, high], axis=1), np.concatenate([low, low], axis=1)], axis=0
        )
        order = np.concatenate([points[::2], points[1::2]])
        up, down = [], []
        for some in (points[::2], points[1::2]):
            cosine, sine = turns(centre[:freqs], some, coarse)
            table = np.concatenate(
                [np.concatenate([cosine, sine], axis=1), np.concatenate([-sine, cosine], axis=1)], axis=0
            )
            for into, piece in ((up, table), (down, table.T)):
                pair = both(piece, 1)
                into.append(np.concatenate([pair, pair], axis=0))
        out["up_cols"], out["down_cols"] = np.stack(up), np.stack(down)
        spread = (np.arange(TS) + HALO)[:, None] - (PAD // coarse) * points[None, :]
        weave = np.ones(spread.shape)
        for p in range(1, freqs):
            weave = weave + 2.0 * np.cos(2.0 * np.pi * np.mod(p * spread, PAD) / PAD)
        weave = weave / coarse
        out["weave_rows"] = both(weave, 1)
        out["weave_cols"] = both(weave[:, order], 1)
        turned = both(weave[:, order].T, 1)
        out["weave_up"] = np.concatenate([turned, turned], axis=0)
        out["weave_down"] = both(weave.T, 0)
        blocks = []
        for j in range(self.n_src):
            pieces = []
            for c in range(self.tile_cols):
                place = np.arange(j * self.width, (j + 1) * self.width) - c * TS + HALO
                inside = ((place >= 0) & (place < PAD)).astype(np.float64)[:, None] * used
                cosine = np.zeros((self.wide, band))
                sine = np.zeros((self.wide, band))
                cosine[: self.width], sine[: self.width] = turns(place, centre, PAD)
                cosine[: self.width] *= inside
                sine[: self.width] *= inside
                pieces.append(
                    np.concatenate([fold(cosine, -sine), fold(sine, cosine)], axis=0).T
                )
            blocks.append(both(np.concatenate(pieces, axis=0), 1))
        out["final_cols"] = np.stack(blocks)
        return {name: np.ascontiguousarray(value) for name, value in out.items()}


def skewed(stages, count, gap):
    for step in range(count + gap * (len(stages) - 1)):
        for late, stage in reversed(list(enumerate(stages))):
            if 0 <= step - late * gap < count:
                stage(step - late * gap)


def image_kernel(plan, names, shift, weight, pupil, mask, target, halo, *refs):
    tabs = dict(zip(names, refs[: len(names)]))
    own_out, row_out = refs[len(names) : len(names) + 2]
    (
        mask_v, target_v, e_rim, final_tab, pupils, spectrum, fields, grads, whole_grad,
        u_high, u_low, woven, lifts, lines, sems,
    ) = refs[len(names) + 2 :]
    sources, group = plan.sources, plan.group
    freqs, reach, band, coarse = plan.freqs, plan.reach, plan.band, plan.coarse
    tile_row = lax.axis_index("tile")
    block = lax.axis_index("src")
    copies = [
        pltpu.make_async_copy(mask, mask_v, sems.at[0]),
        pltpu.make_async_copy(tabs["e_rim"].at[tile_row], e_rim, sems.at[1]),
        pltpu.make_async_copy(target, target_v, sems.at[2]),
        pltpu.make_async_copy(tabs["final_cols"].at[block], final_tab, sems.at[3]),
    ]
    for copy in copies:
        copy.start()
    total = weight[0]
    for s in range(1, sources):
        total = total + weight[s]
    share = 1.0 / total
    lane = lax.broadcasted_iota(jnp.int32, (1, band), 1)
    first_half = lane < freqs
    residue = jnp.where(first_half, lane, lane - freqs)
    sign = jnp.where(first_half, 1.0, -1.0).astype(f32)
    doubled = jnp.concatenate([pupil[...], pupil[...]], axis=1)

    def place_pupil(s):
        pupils[s] = pltpu.roll(doubled, shift[1, s] + reach, 1)

    if sources <= MOST:
        for s in range(sources):
            place_pupil(s)
    else:
        lax.fori_loop(0, sources, lambda s, c: (place_pupil(s), c)[1], 0)

    copies[0].wait()
    copies[1].wait()
    e_own, rim_table = tabs["e_own"], e_rim[...]
    for n in range(0, plan.cols, 256):
        high, low = split(mask_v[:, n : n + 256])
        rim_high, rim_low = split(halo[:, n : n + 256])
        part = dot(e_own[...], high) + dot(rim_table, rim_high)
        rows = part[: 2 * band] + part[2 * band :]
        rows = rows + dot(e_own[: 2 * band, :], low) + dot(rim_table[: 2 * band], rim_low)
        high, low = split(rows)
        u_high[:, n : n + 256] = high
        u_low[:, n : n + 256] = low
    scale = 1.0 / (PAD * PAD)
    for c, (first, last) in enumerate(plan.spans):
        high = jnp.concatenate([u_high[:band, first:last], u_high[band:, first:last]], axis=1)
        low = jnp.concatenate([u_low[:band, first:last], u_low[band:, first:last]], axis=1)
        prod = dot(high, tabs[f"col{c}"][...])
        prod = prod[:, : 2 * band] + prod[:, 2 * band :] + dot(low, tabs[f"col{c}"][:, : 2 * band])
        prod = prod * scale
        for k in range(2):
            half = prod[:, k * band : (k + 1) * band]
            spectrum[c, k] = half
            spectrum[c, 2 + k] = pltpu.roll(half, freqs, 1) * sign

    def lane_block(value, k):
        return value[:, k * band : (k + 1) * band]

    pairs = group // 2

    def forward(c, first, power):
        state = {"p": power}
        keep = c % plan.stores

        def gather(i):
            for k in (2 * i, 2 * i + 1):
                down = shift[0, first + k] + reach
                along = shift[1, first + k] + reach
                rows = pl.ds(down, freqs)
                near = residue >= along
                upper = jnp.where(near, spectrum[c, 0, rows, :], spectrum[c, 1, rows, :])
                lower = jnp.where(near, spectrum[c, 2, rows, :], spectrum[c, 3, rows, :])
                scaled = pupils[first + k]
                high, low = split(jnp.concatenate([upper * scaled, lower * scaled], axis=0))
                lifts[:band, k * band : (k + 1) * band] = high
                lifts[band:, k * band : (k + 1) * band] = low

        def lift(i):
            lifted = dot(tabs["up_rows"][...], lifts[:, 2 * i * band : 2 * (i + 1) * band])
            high, low = split(lifted[:coarse] + lifted[coarse:])
            for k in range(2):
                lines[2 * i + k, :, :band] = lane_block(high, k)
                lines[2 * i + k, :, band:] = lane_block(low, k)

        def light_up(i):
            for k in (2 * i, 2 * i + 1):
                along = shift[1, first + k] + reach
                flip = jnp.where(residue >= along, 1.0, -1.0).astype(bf16)
                line = lines[k]
                even = dot(line, tabs["up_cols"][0])
                odd = dot(line * jnp.concatenate([flip, flip], axis=1), tabs["up_cols"][1])
                field = jnp.concatenate(
                    [even[:, :coarse] + even[:, coarse:], odd[:, :coarse] + odd[:, coarse:]], axis=1
                )
                fields[keep, first + k] = field
                state["p"] = state["p"] + weight[first + k] * (field * field)

        skewed([gather, lift, light_up], pairs, SKEW)
        return state["p"]

    def fine(c, power):
        even, odd = power[:, :coarse], power[:, coarse:]
        power = jnp.where(first_half, even + pltpu.roll(even, freqs, 1), odd + pltpu.roll(odd, freqs, 1))
        high, low = split(power * share)
        power_pair = jnp.concatenate([high, low], axis=1)
        power_quad = jnp.concatenate([power_pair, power_pair], axis=0)
        state = {}

        def rows_of(m):
            return slice(m * FINE, (m + 1) * FINE)

        def weave_rows(m):
            left = dot(tabs["weave_rows"][rows_of(m), :], power_quad)
            high, low = split(left[:, :coarse] + left[:, coarse:])
            state["a", m] = jnp.concatenate([high, low], axis=1)

        def slope_rows(m):
            light = dot(state.pop(("a", m)), tabs["weave_up"][...])
            light = light[:, :TS] + light[:, TS:]
            printed = 1.0 / (1.0 + jnp.exp(-resist_gain * (light - resist_level)))
            wanted = target_v[rows_of(m), c * TS : (c + 1) * TS]
            slope = (2.0 * resist_gain) * (printed - wanted) * printed * (1.0 - printed)
            state["g", m] = split(slope)

        def fold_rows(m):
            high, low = state.pop(("g", m))
            part = dot(high, tabs["weave_cols"][...]) + dot(low, tabs["weave_cols"][...])
            high, low = split(part[:, :coarse] + part[:, coarse:])
            woven[rows_of(m), :] = jnp.concatenate([high, low], axis=1)

        skewed([weave_rows, slope_rows, fold_rows], TS // FINE, 1)
        part = dot(tabs["weave_down"][...], woven[...])
        part = part[:coarse] + part[coarse:]
        pull = (part[:, :coarse] + part[:, coarse:]) * (2.0 * share)
        turned = pltpu.roll(pull, freqs, 1)
        return jnp.concatenate(
            [jnp.where(first_half, pull, turned), jnp.where(first_half, turned, pull)], axis=1
        )

    def backward(c, first, pull):
        keep = c % plan.stores

        def fall(i):
            for k in (2 * i, 2 * i + 1):
                high, low = split(fields[keep, first + k] * (pull * weight[first + k]))
                sums = []
                for h in range(2):
                    left = jnp.concatenate([lane_block(high, h), lane_block(low, h)], axis=1)
                    part = dot(left, tabs["down_cols"][h])
                    sums.append(part[:, :band] + part[:, band:])
                along = shift[1, first + k] + reach
                flip = jnp.where(residue >= along, 1.0, -1.0).astype(f32)
                high, low = split(sums[0] + flip * sums[1])
                lifts[:band, k * band : (k + 1) * band] = high
                lifts[band:, k * band : (k + 1) * band] = low

        def settle(i):
            part = dot(tabs["down_rows"][...], lifts[:, 2 * i * band : 2 * (i + 1) * band])
            part = part[:band] + part[band:]
            for k in range(2):
                s = first + 2 * i + k
                mine = lane_block(part, k)
                mine = (mine[:freqs] + sign * pltpu.roll(mine[freqs:], freqs, 1)) * pupils[s]
                rows = pl.ds(shift[0, s] + reach, freqs)
                near = residue >= shift[1, s] + reach
                zero = jnp.zeros_like(mine)
                grads[c, 0, rows, :] += jnp.where(near, mine, zero)
                grads[c, 1, rows, :] += jnp.where(near, zero, mine)

        skewed([fall, settle], pairs, SKEW)

    copies[2].wait()
    grads[...] = jnp.zeros_like(grads)
    rounds = sources // group
    for c in range(plan.tile_cols):
        power = jnp.zeros((coarse, 2 * coarse), f32)
        if rounds == 1:
            power = forward(c, 0, power)
        else:
            power = lax.fori_loop(0, rounds, lambda g, p: forward(c, g * group, p), power)
        pull = fine(c, power)
        if rounds == 1:
            backward(c, 0, pull)
        else:
            lax.fori_loop(0, rounds, lambda g, n: (backward(c, g * group, pull), n)[1], 0)

    copies[3].wait()
    wide = plan.wide
    bands = jnp.concatenate([grads[c, k] for c in range(plan.tile_cols) for k in range(2)], axis=1) * scale
    high, low = split(bands)
    part = dot(high, final_tab[...])
    part = part[:, : 2 * wide] + part[:, 2 * wide :] + dot(low, final_tab[:, : 2 * wide])
    high, low = split(jnp.concatenate([part[:, :wide], part[:, wide:]], axis=0))
    rows_high, rows_low = tabs["final_rows"][0], tabs["final_rows"][1]
    whole_grad[...] = dot(rows_high, high) + dot(rows_high, low) + dot(rows_low, high)
    own_out[...] = whole_grad[HALO : HALO + TS, : plan.width]
    rim_start = pl.multiple_of(jnp.where(tile_row == 0, HALO + TS, 0), HALO)
    row_out[...] = whole_grad[pl.ds(rim_start, HALO), : plan.width]


def finish_kernel(own, row, out):
    tile_row = lax.axis_index("tile")
    out[...] = own[...]
    first = pl.multiple_of(jnp.where(tile_row == 0, TS - HALO, 0), HALO)
    out[pl.ds(first, HALO), :] += row[...]


def local_image(plan, mask, target, pupil, source_shift, source_weight, halo):
    tables = plan.tables()
    names = tuple(tables)
    vmem = pl.BlockSpec(memory_space=pltpu.VMEM)
    smem = pl.BlockSpec(memory_space=pltpu.SMEM)
    distant = pl.BlockSpec(memory_space=pltpu.MemorySpace.HBM)
    sources, group, tile_cols = plan.sources, plan.group, plan.tile_cols
    band, coarse = plan.band, plan.coarse
    return pl.pallas_call(
        functools.partial(image_kernel, plan, names),
        out_shape=[
            jax.ShapeDtypeStruct((TS, plan.width), f32),
            jax.ShapeDtypeStruct((HALO, plan.width), f32),
        ],
        in_specs=[smem, smem, vmem, distant, distant, vmem]
        + [distant if name in ("e_rim", "final_cols") else vmem for name in names],
        out_specs=[vmem] * 2,
        scratch_shapes=[
            pltpu.VMEM((TS, plan.cols), f32),
            pltpu.VMEM((TS, plan.cols), f32),
            pltpu.VMEM(tables["e_rim"].shape[1:], bf16),
            pltpu.VMEM(tables["final_cols"].shape[1:], bf16),
            pltpu.VMEM((sources, plan.freqs, band), f32),
            pltpu.VMEM((tile_cols, 4, band, band), f32),
            pltpu.VMEM((plan.stores, sources, coarse, 2 * coarse), f32),
            pltpu.VMEM((tile_cols, 2, band, band), f32),
            pltpu.VMEM((PAD, plan.wide), f32),
            pltpu.VMEM((2 * band, plan.cols), bf16),
            pltpu.VMEM((2 * band, plan.cols), bf16),
            pltpu.VMEM((TS, 2 * coarse), bf16),
            pltpu.VMEM((2 * band, group * band), bf16),
            pltpu.VMEM((group, coarse, 2 * band), bf16),
            pltpu.SemaphoreType.DMA((4,)),
        ],
        compiler_params=pltpu.CompilerParams(vmem_limit_bytes=(28 + sources // 8) * 1024 * 1024),
        name="image",
    )(source_shift.T, source_weight, pupil, mask, target, halo, *[jnp.asarray(tables[n]) for n in names])


def shards(plan, mask, target, pupil, source_shift, source_weight):
    tile_row = lax.axis_index("tile")
    swap = [(0, 1), (1, 0)]
    edge = lax.dynamic_slice_in_dim(mask, jnp.where(tile_row == 0, TS - HALO, 0), HALO, 0)
    halo = lax.ppermute(edge, "tile", swap)
    own, row = local_image(plan, mask, target, pupil, source_shift, source_weight, halo)
    row = lax.ppermute(row, "tile", swap)
    vmem = pl.BlockSpec(memory_space=pltpu.VMEM)
    return pl.pallas_call(
        finish_kernel,
        out_shape=jax.ShapeDtypeStruct((TS, plan.width), f32),
        in_specs=[vmem] * 2,
        out_specs=vmem,
        name="finish",
    )(own, row)


def solution(mesh):
    sizes = dict(mesh.shape)

    def run(mask, target, pupil, source_shift, source_weight):
        plan = Plan(pupil.shape[0], mask.shape[1], sizes["src"], source_shift.shape[0])
        placed = (P(("groups", "tile"), None), P(("groups", "tile"), None), P(), P(), P())
        return jax.shard_map(
            functools.partial(shards, plan),
            mesh=mesh,
            in_specs=placed,
            out_specs=P(("groups", "tile"), "src"),
            check_vma=False,
        )(mask, target, pupil, source_shift, source_weight)

    return run
```

```python
import functools
import math

import jax
import jax.numpy as jnp
import ml_dtypes
import numpy as np
from jax import lax
from jax.experimental import pallas as pl
from jax.experimental.pallas import tpu as pltpu
from jax.sharding import PartitionSpec as P

TS = 512
HALO = 64
PAD = TS + 2 * HALO
LANES = 128
SKEW = 12
FINE = 512
MOST = 24

resist_gain = 25.0
resist_level = 0.25

f32 = jnp.float32
bf16 = jnp.bfloat16


def halves(table):
    table = np.asarray(table, np.float64)
    high = table.astype(np.float32).astype(ml_dtypes.bfloat16)
    low = (table - high.astype(np.float64)).astype(np.float32).astype(ml_dtypes.bfloat16)
    return high, low


def turns(left, right, period):
    angle = 2.0 * np.pi * np.mod(np.outer(left, right), period) / period
    return np.cos(angle), np.sin(angle)


def both(table, axis):
    return np.concatenate(halves(table), axis=axis)


def split(value):
    high = value.astype(bf16)
    return high, (value - high.astype(f32)).astype(bf16)


def dot(left, right):
    return lax.dot_general(left, right, (((1,), (0,)), ((), ())), preferred_element_type=f32)


class Plan:
    def __init__(self, freqs, cols, n_src, sources):
        self.freqs = freqs
        self.reach = (3 * freqs) // 8
        self.band = 2 * freqs
        self.coarse = 2 * freqs
        self.cols = cols
        self.tile_cols = cols // TS
        self.width = cols // n_src
        self.wide = -(-self.width // LANES) * LANES
        self.n_src = n_src
        self.sources = sources
        self.group = max(n for n in range(2, MOST + 1, 2) if sources % n == 0)
        self.stores = self.tile_cols if sources <= MOST else 1
        self.spans = [
            (max(0, c * TS - LANES), min(cols, (c + 1) * TS + LANES)) for c in range(self.tile_cols)
        ]

    def tables(self):
        freqs, band, coarse = self.freqs, self.band, self.coarse
        index = np.arange(band)
        used = (index < freqs + 2 * self.reach).astype(np.float64)
        centre = index - (freqs // 2 + self.reach)
        out = {}
        cosine, sine = turns(centre, np.arange(PAD), PAD)
        rows = np.concatenate([cosine, -sine], axis=0) * np.concatenate([used, used])[:, None]
        out["e_own"] = both(rows[:, HALO : HALO + TS], 0)
        out["e_rim"] = np.stack([both(rows[:, HALO + TS :], 0), both(rows[:, :HALO], 0)])
        out["final_rows"] = np.stack(halves(rows.T))

        def fold(real, imag):
            return np.concatenate(
                [real[:, :freqs], imag[:, :freqs], real[:, freqs:], imag[:, freqs:]], axis=1
            )

        for c, (first, last) in enumerate(self.spans):
            place = np.arange(first, last) - c * TS + HALO
            inside = ((place >= 0) & (place < PAD)).astype(np.float64)[:, None] * used
            cosine, sine = turns(place, centre, PAD)
            cosine, sine = cosine * inside, sine * inside
            out[f"col{c}"] = both(np.concatenate([fold(cosine, -sine), fold(sine, cosine)], axis=0), 1)
        relative = np.arange(freqs) - freqs // 2
        points = np.arange(coarse)
        cosine, sine = turns(points, relative, coarse)
        high, low = halves(np.concatenate([cosine, -sine], axis=1))
        out["up_rows"] = np.concatenate(
            [np.concatenate([high, high], axis=1), np.concatenate([low, low], axis=1)], axis=0
        )
        high, low = halves(np.concatenate([cosine.T, sine.T], axis=0))
        out["down_rows"] = np.concatenate(
            [np.concatenate([high, high], axis=1), np.concatenate([low, low], axis=1)], axis=0
        )
        order = np.concatenate([points[::2], points[1::2]])
        up, down = [], []
        for some in (points[::2], points[1::2]):
            cosine, sine = turns(centre[:freqs], some, coarse)
            table = np.concatenate(
                [np.concatenate([cosine, sine], axis=1), np.concatenate([-sine, cosine], axis=1)], axis=0
            )
            for into, piece in ((up, table), (down, table.T)):
                pair = both(piece, 1)
                into.append(np.concatenate([pair, pair], axis=0))
        out["up_cols"], out["down_cols"] = np.stack(up), np.stack(down)
        spread = (np.arange(TS) + HALO)[:, None] - (PAD // coarse) * points[None, :]
        weave = np.ones(spread.shape)
        for p in range(1, freqs):
            weave = weave + 2.0 * np.cos(2.0 * np.pi * np.mod(p * spread, PAD) / PAD)
        weave = weave / coarse
        out["weave_rows"] = both(weave, 1)
        out["weave_cols"] = both(weave[:, order], 1)
        turned = both(weave[:, order].T, 1)
        out["weave_up"] = np.concatenate([turned, turned], axis=0)
        out["weave_down"] = both(weave.T, 0)
        blocks = []
        for j in range(self.n_src):
            pieces = []
            for c in range(self.tile_cols):
                place = np.arange(j * self.width, (j + 1) * self.width) - c * TS + HALO
                inside = ((place >= 0) & (place < PAD)).astype(np.float64)[:, None] * used
                cosine = np.zeros((self.wide, band))
                sine = np.zeros((self.wide, band))
                cosine[: self.width], sine[: self.width] = turns(place, centre, PAD)
                cosine[: self.width] *= inside
                sine[: self.width] *= inside
                pieces.append(
                    np.concatenate([fold(cosine, -sine), fold(sine, cosine)], axis=0).T
                )
            blocks.append(both(np.concatenate(pieces, axis=0), 1))
        out["final_cols"] = np.stack(blocks)
        return {name: np.ascontiguousarray(value) for name, value in out.items()}


def skewed(stages, count, gap):
    for step in range(count + gap * (len(stages) - 1)):
        for late, stage in reversed(list(enumerate(stages))):
            if 0 <= step - late * gap < count:
                stage(step - late * gap)


def image_kernel(plan, names, shift, weight, *refs):
    far = dict(zip(names, refs[: len(names)]))
    own_out, row_out = refs[len(names) : len(names) + 2]
    near = dict(zip(names, refs[len(names) + 2 :]))
    (
        pupils, spectrum, fields, grads, whole_grad, u_high, u_low, woven, lifts, lines, sems,
    ) = refs[2 * len(names) + 2 :]
    sources, group = plan.sources, plan.group
    freqs, reach, band, coarse = plan.freqs, plan.reach, plan.band, plan.coarse
    tile_row = lax.axis_index("tile")
    block = lax.axis_index("src")
    picked = {"e_rim": tile_row, "final_cols": block}
    pending = {}
    for i, name in enumerate(names):
        source = far[name].at[picked[name]] if name in picked else far[name]
        pending[name] = pltpu.make_async_copy(source, near[name], sems.at[i])
        pending[name].start()

    def need(*wanted):
        for name in wanted:
            if name in pending:
                pending.pop(name).wait()

    tabs = near
    mask_v, target_v, e_rim, final_tab, halo = (
        near[name] for name in ("mask", "target", "e_rim", "final_cols", "halo")
    )
    total = weight[0]
    for s in range(1, sources):
        total = total + weight[s]
    share = 1.0 / total
    lane = lax.broadcasted_iota(jnp.int32, (1, band), 1)
    first_half = lane < freqs
    residue = jnp.where(first_half, lane, lane - freqs)
    sign = jnp.where(first_half, 1.0, -1.0).astype(f32)
    need("pupil")
    doubled = jnp.concatenate([near["pupil"][...]] * 2, axis=1)

    def place_pupil(s):
        pupils[s] = pltpu.roll(doubled, shift[1, s] + reach, 1)

    if sources <= MOST:
        for s in range(sources):
            place_pupil(s)
    else:
        lax.fori_loop(0, sources, lambda s, c: (place_pupil(s), c)[1], 0)

    need("mask", "e_own", "e_rim", "halo")
    e_own, rim_table = tabs["e_own"], e_rim[...]
    for n in range(0, plan.cols, 256):
        high, low = split(mask_v[:, n : n + 256])
        rim_high, rim_low = split(halo[:, n : n + 256])
        part = dot(e_own[...], high) + dot(rim_table, rim_high)
        rows = part[: 2 * band] + part[2 * band :]
        rows = rows + dot(e_own[: 2 * band, :], low) + dot(rim_table[: 2 * band], rim_low)
        high, low = split(rows)
        u_high[:, n : n + 256] = high
        u_low[:, n : n + 256] = low
    scale = 1.0 / (PAD * PAD)
    for c, (first, last) in enumerate(plan.spans):
        need(f"col{c}")
        high = jnp.concatenate([u_high[:band, first:last], u_high[band:, first:last]], axis=1)
        low = jnp.concatenate([u_low[:band, first:last], u_low[band:, first:last]], axis=1)
        prod = dot(high, tabs[f"col{c}"][...])
        prod = prod[:, : 2 * band] + prod[:, 2 * band :] + dot(low, tabs[f"col{c}"][:, : 2 * band])
        prod = prod * scale
        for k in range(2):
            half = prod[:, k * band : (k + 1) * band]
            spectrum[c, k] = half
            spectrum[c, 2 + k] = pltpu.roll(half, freqs, 1) * sign

    def lane_block(value, k):
        return value[:, k * band : (k + 1) * band]

    pairs = group // 2

    def forward(c, first, power):
        state = {"p": power}
        keep = c % plan.stores

        def gather(i):
            for k in (2 * i, 2 * i + 1):
                down = shift[0, first + k] + reach
                along = shift[1, first + k] + reach
                rows = pl.ds(down, freqs)
                near = residue >= along
                upper = jnp.where(near, spectrum[c, 0, rows, :], spectrum[c, 1, rows, :])
                lower = jnp.where(near, spectrum[c, 2, rows, :], spectrum[c, 3, rows, :])
                scaled = pupils[first + k]
                high, low = split(jnp.concatenate([upper * scaled, lower * scaled], axis=0))
                lifts[:band, k * band : (k + 1) * band] = high
                lifts[band:, k * band : (k + 1) * band] = low

        def lift(i):
            lifted = dot(tabs["up_rows"][...], lifts[:, 2 * i * band : 2 * (i + 1) * band])
            high, low = split(lifted[:coarse] + lifted[coarse:])
            for k in range(2):
                lines[2 * i + k, :, :band] = lane_block(high, k)
                lines[2 * i + k, :, band:] = lane_block(low, k)

        def light_up(i):
            for k in (2 * i, 2 * i + 1):
                along = shift[1, first + k] + reach
                flip = jnp.where(residue >= along, 1.0, -1.0).astype(bf16)
                line = lines[k]
                even = dot(line, tabs["up_cols"][0])
                odd = dot(line * jnp.concatenate([flip, flip], axis=1), tabs["up_cols"][1])
                field = jnp.concatenate(
                    [even[:, :coarse] + even[:, coarse:], odd[:, :coarse] + odd[:, coarse:]], axis=1
                )
                fields[keep, first + k] = field
                state["p"] = state["p"] + weight[first + k] * (field * field)

        skewed([gather, lift, light_up], pairs, SKEW)
        return state["p"]

    def fine(c, power):
        even, odd = power[:, :coarse], power[:, coarse:]
        power = jnp.where(first_half, even + pltpu.roll(even, freqs, 1), odd + pltpu.roll(odd, freqs, 1))
        high, low = split(power * share)
        power_pair = jnp.concatenate([high, low], axis=1)
        power_quad = jnp.concatenate([power_pair, power_pair], axis=0)
        state = {}

        def rows_of(m):
            return slice(m * FINE, (m + 1) * FINE)

        def weave_rows(m):
            left = dot(tabs["weave_rows"][rows_of(m), :], power_quad)
            high, low = split(left[:, :coarse] + left[:, coarse:])
            state["a", m] = jnp.concatenate([high, low], axis=1)

        def slope_rows(m):
            light = dot(state.pop(("a", m)), tabs["weave_up"][...])
            light = light[:, :TS] + light[:, TS:]
            printed = 1.0 / (1.0 + jnp.exp(-resist_gain * (light - resist_level)))
            wanted = target_v[rows_of(m), c * TS : (c + 1) * TS]
            slope = (2.0 * resist_gain) * (printed - wanted) * printed * (1.0 - printed)
            state["g", m] = split(slope)

        def fold_rows(m):
            high, low = state.pop(("g", m))
            part = dot(high, tabs["weave_cols"][...]) + dot(low, tabs["weave_cols"][...])
            high, low = split(part[:, :coarse] + part[:, coarse:])
            woven[rows_of(m), :] = jnp.concatenate([high, low], axis=1)

        skewed([weave_rows, slope_rows, fold_rows], TS // FINE, 1)
        part = dot(tabs["weave_down"][...], woven[...])
        part = part[:coarse] + part[coarse:]
        pull = (part[:, :coarse] + part[:, coarse:]) * (2.0 * share)
        turned = pltpu.roll(pull, freqs, 1)
        return jnp.concatenate(
            [jnp.where(first_half, pull, turned), jnp.where(first_half, turned, pull)], axis=1
        )

    def backward(c, first, pull):
        keep = c % plan.stores

        def fall(i):
            for k in (2 * i, 2 * i + 1):
                high, low = split(fields[keep, first + k] * (pull * weight[first + k]))
                sums = []
                for h in range(2):
                    left = jnp.concatenate([lane_block(high, h), lane_block(low, h)], axis=1)
                    part = dot(left, tabs["down_cols"][h])
                    sums.append(part[:, :band] + part[:, band:])
                along = shift[1, first + k] + reach
                flip = jnp.where(residue >= along, 1.0, -1.0).astype(f32)
                high, low = split(sums[0] + flip * sums[1])
                lifts[:band, k * band : (k + 1) * band] = high
                lifts[band:, k * band : (k + 1) * band] = low

        def settle(i):
            part = dot(tabs["down_rows"][...], lifts[:, 2 * i * band : 2 * (i + 1) * band])
            part = part[:band] + part[band:]
            for k in range(2):
                s = first + 2 * i + k
                mine = lane_block(part, k)
                mine = (mine[:freqs] + sign * pltpu.roll(mine[freqs:], freqs, 1)) * pupils[s]
                rows = pl.ds(shift[0, s] + reach, freqs)
                near = residue >= shift[1, s] + reach
                zero = jnp.zeros_like(mine)
                grads[c, 0, rows, :] += jnp.where(near, mine, zero)
                grads[c, 1, rows, :] += jnp.where(near, zero, mine)

        skewed([fall, settle], pairs, SKEW)

    need("up_rows", "up_cols")
    grads[...] = jnp.zeros_like(grads)
    rounds = sources // group
    for c in range(plan.tile_cols):
        power = jnp.zeros((coarse, 2 * coarse), f32)
        if rounds == 1:
            power = forward(c, 0, power)
        else:
            power = lax.fori_loop(0, rounds, lambda g, p: forward(c, g * group, p), power)
        need("target", "weave_rows", "weave_up", "weave_cols", "weave_down")
        pull = fine(c, power)
        need("down_rows", "down_cols")
        if rounds == 1:
            backward(c, 0, pull)
        else:
            lax.fori_loop(0, rounds, lambda g, n: (backward(c, g * group, pull), n)[1], 0)

    need("final_cols", "final_rows")
    wide = plan.wide
    bands = jnp.concatenate([grads[c, k] for c in range(plan.tile_cols) for k in range(2)], axis=1) * scale
    high, low = split(bands)
    part = dot(high, final_tab[...])
    part = part[:, : 2 * wide] + part[:, 2 * wide :] + dot(low, final_tab[:, : 2 * wide])
    high, low = split(jnp.concatenate([part[:, :wide], part[:, wide:]], axis=0))
    rows_high, rows_low = tabs["final_rows"][0], tabs["final_rows"][1]
    final = dot(rows_high, high) + dot(rows_high, low) + dot(rows_low, high)
    whole_grad[...] = final[:, : plan.width]
    rim_start = pl.multiple_of(jnp.where(tile_row == 0, HALO + TS, 0), HALO)
    ends = [
        pltpu.make_async_copy(whole_grad.at[pl.ds(rim_start, HALO)], row_out, sems.at[0]),
        pltpu.make_async_copy(whole_grad.at[pl.ds(HALO, TS)], own_out, sems.at[1]),
    ]
    for end in ends:
        end.start()
    for end in ends:
        end.wait()


def finish_kernel(own, row, out, mine, other, sems):
    tile_row = lax.axis_index("tile")
    first = pl.multiple_of(jnp.where(tile_row == 0, TS - HALO, 0), HALO)
    rows = pl.ds(first, HALO)
    loads = [
        pltpu.make_async_copy(out.at[rows], mine, sems.at[0]),
        pltpu.make_async_copy(row, other, sems.at[1]),
    ]
    for load in loads:
        load.start()
    for load in loads:
        load.wait()
    mine[...] = mine[...] + other[...]
    store = pltpu.make_async_copy(mine, out.at[rows], sems.at[0])
    store.start()
    store.wait()


def local_image(plan, mask, target, pupil, source_shift, source_weight, halo):
    tables = plan.tables()
    arrays = {"mask": mask, "e_own": tables["e_own"], "e_rim": tables["e_rim"], "pupil": pupil}
    arrays.update(halo=halo, **{n: t for n, t in tables.items() if n not in arrays}, target=target)
    names = tuple(arrays)
    picked = ("e_rim", "final_cols")
    local = {n: a.shape[1:] if n in picked else a.shape for n, a in arrays.items()}
    smem = pl.BlockSpec(memory_space=pltpu.SMEM)
    distant = pl.BlockSpec(memory_space=pltpu.MemorySpace.HBM)
    sources, group, tile_cols = plan.sources, plan.group, plan.tile_cols
    band, coarse = plan.band, plan.coarse
    return pl.pallas_call(
        functools.partial(image_kernel, plan, names),
        out_shape=[
            jax.ShapeDtypeStruct((TS, plan.width), f32),
            jax.ShapeDtypeStruct((HALO, plan.width), f32),
        ],
        in_specs=[smem, smem] + [distant] * len(names),
        out_specs=[distant] * 2,
        scratch_shapes=[pltpu.VMEM(local[n], arrays[n].dtype) for n in names]
        + [
            pltpu.VMEM((sources, plan.freqs, band), f32),
            pltpu.VMEM((tile_cols, 4, band, band), f32),
            pltpu.VMEM((plan.stores, sources, coarse, 2 * coarse), f32),
            pltpu.VMEM((tile_cols, 2, band, band), f32),
            pltpu.VMEM((PAD, plan.width), f32),
            pltpu.VMEM((2 * band, plan.cols), bf16),
            pltpu.VMEM((2 * band, plan.cols), bf16),
            pltpu.VMEM((TS, 2 * coarse), bf16),
            pltpu.VMEM((2 * band, group * band), bf16),
            pltpu.VMEM((group, coarse, 2 * band), bf16),
            pltpu.SemaphoreType.DMA((len(names),)),
        ],
        compiler_params=pltpu.CompilerParams(vmem_limit_bytes=60 * 1024 * 1024),
        name="image",
    )(source_shift.T, source_weight, *[jnp.asarray(arrays[n]) for n in names])


def shards(plan, mask, target, pupil, source_shift, source_weight):
    tile_row = lax.axis_index("tile")
    swap = [(0, 1), (1, 0)]
    edge = lax.dynamic_slice_in_dim(mask, jnp.where(tile_row == 0, TS - HALO, 0), HALO, 0)
    halo = lax.ppermute(edge, "tile", swap)
    own, row = local_image(plan, mask, target, pupil, source_shift, source_weight, halo)
    row = lax.ppermute(row, "tile", swap)
    distant = pl.BlockSpec(memory_space=pltpu.MemorySpace.HBM)
    piece = pltpu.VMEM((HALO, plan.width), f32)
    return pl.pallas_call(
        finish_kernel,
        out_shape=jax.ShapeDtypeStruct((TS, plan.width), f32),
        in_specs=[distant, pl.BlockSpec(memory_space=pl.ANY)],
        out_specs=distant,
        scratch_shapes=[piece, piece, pltpu.SemaphoreType.DMA((2,))],
        input_output_aliases={0: 0},
        name="finish",
    )(own, row)


def solution(mesh):
    sizes = dict(mesh.shape)

    def run(mask, target, pupil, source_shift, source_weight):
        plan = Plan(pupil.shape[0], mask.shape[1], sizes["src"], source_shift.shape[0])
        placed = (P(("groups", "tile"), None), P(("groups", "tile"), None), P(), P(), P())
        return jax.shard_map(
            functools.partial(shards, plan),
            mesh=mesh,
            in_specs=placed,
            out_specs=P(("groups", "tile"), "src"),
            check_vma=False,
        )(mask, target, pupil, source_shift, source_weight)

    return run
```

```python
import functools
import math

import jax
import jax.numpy as jnp
import ml_dtypes
import numpy as np
from jax import lax
from jax.experimental import pallas as pl
from jax.experimental.pallas import tpu as pltpu
from jax.sharding import PartitionSpec as P

TS = 512
HALO = 64
PAD = TS + 2 * HALO
LANES = 128
FINE = 256
CHUNK = 1024
LAG = 1
MOST = 24

resist_gain = 25.0
resist_level = 0.25

f32 = jnp.float32
bf16 = jnp.bfloat16


def halves(table):
    table = np.asarray(table, np.float64)
    high = table.astype(np.float32).astype(ml_dtypes.bfloat16)
    low = (table - high.astype(np.float64)).astype(np.float32).astype(ml_dtypes.bfloat16)
    return high, low


def turns(left, right, period):
    angle = 2.0 * np.pi * np.mod(np.outer(left, right), period) / period
    return np.cos(angle), np.sin(angle)


def both(table, axis):
    return np.concatenate(halves(table), axis=axis)


def split(value):
    high = value.astype(bf16)
    return high, (value - high.astype(f32)).astype(bf16)


def dot(left, right):
    return lax.dot_general(left, right, (((1,), (0,)), ((), ())), preferred_element_type=f32)


class Plan:
    def __init__(self, freqs, cols, n_src, sources):
        self.freqs = freqs
        self.reach = (3 * freqs) // 8
        self.band = 2 * freqs
        self.coarse = 2 * freqs
        self.cols = cols
        self.tile_cols = cols // TS
        self.width = cols // n_src
        self.wide = -(-self.width // LANES) * LANES
        self.n_src = n_src
        self.sources = sources
        self.group = max(n for n in range(2, MOST + 1, 2) if sources % n == 0)
        self.stores = self.tile_cols if sources <= MOST else 1
        self.spans = [
            (max(0, c * TS - LANES), min(cols, (c + 1) * TS + LANES)) for c in range(self.tile_cols)
        ]

    def tables(self):
        freqs, band, coarse = self.freqs, self.band, self.coarse
        index = np.arange(band)
        used = (index < freqs + 2 * self.reach).astype(np.float64)
        centre = index - (freqs // 2 + self.reach)
        out = {}
        cosine, sine = turns(centre, np.arange(PAD), PAD)
        rows = np.concatenate([cosine, -sine], axis=0) * np.concatenate([used, used])[:, None]
        out["e_own"] = both(rows[:, HALO : HALO + TS], 0)
        rims = []
        for rim in (rows[:, HALO + TS :], rows[:, :HALO]):
            high, low = halves(rim)
            rims.append(np.concatenate([high, low, high], axis=1))
        out["e_rim"] = np.stack(rims)

        def fold(real, imag):
            return np.concatenate(
                [real[:, :freqs], imag[:, :freqs], real[:, freqs:], imag[:, freqs:]], axis=1
            )

        place = np.arange(-LANES, TS + LANES) + HALO
        inside = ((place >= 0) & (place < PAD)).astype(np.float64)[:, None] * used
        cosine, sine = turns(place, centre, PAD)
        out["cols"] = both(fold(cosine * inside, -sine * inside), 1)
        relative = np.arange(freqs) - freqs // 2
        points = np.arange(coarse)
        cosine, sine = turns(points, relative, coarse)
        high, low = halves(np.concatenate([cosine, -sine], axis=1))
        out["up_rows"] = np.concatenate(
            [np.concatenate([high, high], axis=1), np.concatenate([low, low], axis=1)], axis=0
        )
        high, low = halves(np.concatenate([cosine.T, sine.T], axis=0))
        out["down_rows"] = np.concatenate(
            [np.concatenate([high, high], axis=1), np.concatenate([low, low], axis=1)], axis=0
        )
        order = np.concatenate([points[::2], points[1::2]])
        up, down = [], []
        for some in (points[::2], points[1::2]):
            cosine, sine = turns(centre[:freqs], some, coarse)
            table = np.concatenate(
                [np.concatenate([cosine, sine], axis=1), np.concatenate([-sine, cosine], axis=1)], axis=0
            )
            for into, piece in ((up, table), (down, table.T)):
                pair = both(piece, 1)
                into.append(np.concatenate([pair, pair], axis=0))
        out["up_cols"], out["down_cols"] = np.stack(up), np.stack(down)
        spread = (np.arange(TS) + HALO)[:, None] - (PAD // coarse) * points[None, :]
        weave = np.ones(spread.shape)
        for p in range(1, freqs):
            weave = weave + 2.0 * np.cos(2.0 * np.pi * np.mod(p * spread, PAD) / PAD)
        weave = weave / coarse
        out["weave_rows"] = both(weave, 1)
        out["weave_cols"] = both(weave[:, order], 1)
        turned = both(weave[:, order].T, 1)
        out["weave_up"] = np.concatenate([turned, turned], axis=0)
        out["weave_down"] = both(weave.T, 0)
        blocks = []
        for j in range(self.n_src):
            pieces = []
            for c in range(self.tile_cols):
                place = np.arange(j * self.width, (j + 1) * self.width) - c * TS + HALO
                inside = ((place >= 0) & (place < PAD)).astype(np.float64)[:, None] * used
                cosine = np.zeros((self.wide, band))
                sine = np.zeros((self.wide, band))
                cosine[: self.width], sine[: self.width] = turns(place, centre, PAD)
                cosine[: self.width] *= inside
                sine[: self.width] *= inside
                pieces.append(
                    np.concatenate([fold(cosine, -sine), fold(sine, cosine)], axis=0).T
                )
            blocks.append(both(np.concatenate(pieces, axis=0), 1))
        out["final_cols"] = np.stack(blocks)
        out["final_rows"] = np.stack(halves(rows.T))
        return {name: np.ascontiguousarray(value) for name, value in out.items()}


def merged(*lists):
    keyed = [((i + 0.5) / len(steps), n, step) for n, steps in enumerate(lists) for i, step in enumerate(steps)]
    return [step for _, _, step in sorted(keyed, key=lambda item: item[:2])]


def run(steps):
    for step in steps:
        step()


def image_kernel(plan, names, shift, weight, *refs):
    far = dict(zip(names, refs[: len(names)]))
    own_out, row_out = refs[len(names) : len(names) + 2]
    near = dict(zip(names, refs[len(names) + 2 :]))
    (
        pupils, spectrum, fields, grads, whole_grad, u_high, u_low, woven, lifts, lines, sems,
    ) = refs[2 * len(names) + 2 :]
    sources, group = plan.sources, plan.group
    freqs, reach, band, coarse = plan.freqs, plan.reach, plan.band, plan.coarse
    tile_row = lax.axis_index("tile")
    block = lax.axis_index("src")
    picked = {"e_rim": tile_row, "final_cols": block}
    pending = {}
    for i, name in enumerate(names):
        source = far[name].at[picked[name]] if name in picked else far[name]
        if name.startswith("mask"):
            source = far[name].at[:, pl.ds(int(name[4:]) * CHUNK, CHUNK)]
        pending[name] = pltpu.make_async_copy(source, near[name], sems.at[i])
    early = ("pupil", "e_own", "e_rim", "halo", "cols")
    started = [name for name in names if name in early or name.startswith("mask")]
    for name in started:
        pending[name].start()

    def need(*wanted):
        for name in wanted:
            if name in pending:
                pending.pop(name).wait()

    tabs = near
    target_v, e_rim, final_tab, halo = (
        near[name] for name in ("target", "e_rim", "final_cols", "halo")
    )
    total = weight[0]
    for s in range(1, sources):
        total = total + weight[s]
    scale = 1.0 / (PAD * PAD)
    lane = lax.broadcasted_iota(jnp.int32, (1, band), 1)
    first_half = lane < freqs
    residue = jnp.where(first_half, lane, lane - freqs)
    sign = jnp.where(first_half, 1.0, -1.0).astype(f32)
    need("pupil")
    doubled = jnp.concatenate([near["pupil"][...]] * 2, axis=1)

    def place_pupil(s):
        strength = jnp.sqrt(jnp.full((1, band), weight[s] / total, f32)) * scale
        pupils[s] = pltpu.roll(doubled, shift[1, s] + reach, 1) * strength

    if sources <= MOST:
        for s in range(sources):
            place_pupil(s)
    else:
        lax.fori_loop(0, sources, lambda s, c: (place_pupil(s), c)[1], 0)

    need("e_own", "e_rim", "halo")
    e_own, rim_table = tabs["e_own"], e_rim[...]
    for i in range(0, plan.cols // CHUNK):
        cols = slice(i * CHUNK, (i + 1) * CHUNK)
        need(f"mask{i}")
        if i == 0:
            for name in names:
                if name not in started:
                    pending[name].start()
        high, low = split(near[f"mask{i}"][...])
        rim_high, rim_low = split(halo[:, cols])
        rows = dot(rim_table, jnp.concatenate([rim_high, rim_high, rim_low], axis=0))
        part = dot(e_own[...], high)
        rows = rows + part[: 2 * band] + part[2 * band :] + dot(e_own[: 2 * band, :], low)
        high, low = split(rows)
        u_high[:, cols] = high
        u_low[:, cols] = low
    need("cols")

    def transform(c):
        first, last = plan.spans[c]
        inside = slice(first - c * TS + LANES, last - c * TS + LANES)
        prod = dot(u_high[:, first:last], tabs["cols"][inside, :])
        prod = prod[:, : 2 * band] + prod[:, 2 * band :]
        prod = prod + dot(u_low[:, first:last], tabs["cols"][inside, : 2 * band])
        for k in range(2):
            own, other = prod[:band, k * band : (k + 1) * band], prod[band:, k * band : (k + 1) * band]
            half = own - sign * pltpu.roll(other, freqs, 1)
            spectrum[c, k] = half
            spectrum[c, 2 + k] = pltpu.roll(half, freqs, 1) * sign

    def lane_block(value, k):
        return value[:, k * band : (k + 1) * band]

    pairs = group // 2
    state = {}

    def gather(c, first, i):
        for k in (2 * i, 2 * i + 1):
            down = shift[0, first + k] + reach
            along = shift[1, first + k] + reach
            rows = pl.ds(down, freqs)
            close = residue >= along
            upper = jnp.where(close, spectrum[c, 0, rows, :], spectrum[c, 1, rows, :])
            lower = jnp.where(close, spectrum[c, 2, rows, :], spectrum[c, 3, rows, :])
            scaled = pupils[first + k]
            high, low = split(jnp.concatenate([upper * scaled, lower * scaled], axis=0))
            lifts[c, :band, k * band : (k + 1) * band] = high
            lifts[c, band:, k * band : (k + 1) * band] = low

    def lift(c, first, i):
        lifted = dot(tabs["up_rows"][...], lifts[c, :, 2 * i * band : 2 * (i + 1) * band])
        high, low = split(lifted[:coarse] + lifted[coarse:])
        for k in range(2):
            lines[c, 2 * i + k, :, :band] = lane_block(high, k)
            lines[c, 2 * i + k, :, band:] = lane_block(low, k)

    def light_up(c, first, i):
        for k in (2 * i, 2 * i + 1):
            along = shift[1, first + k] + reach
            flip = jnp.where(residue >= along, 1.0, -1.0).astype(bf16)
            line = lines[c, k]
            even = dot(line, tabs["up_cols"][0])
            odd = dot(line * jnp.concatenate([flip, flip], axis=1), tabs["up_cols"][1])
            field = jnp.concatenate(
                [even[:, :coarse] + even[:, coarse:], odd[:, :coarse] + odd[:, coarse:]], axis=1
            )
            fields[c % plan.stores, first + k] = field
            state["power", c] = state["power", c] + field * field

    def fine_steps(c):
        def begin():
            power = state.pop(("power", c))
            even, odd = power[:, :coarse], power[:, coarse:]
            power = jnp.where(first_half, even + pltpu.roll(even, freqs, 1), odd + pltpu.roll(odd, freqs, 1))
            high, low = split(power)
            pair = jnp.concatenate([high, low], axis=1)
            state["quad", c] = jnp.concatenate([pair, pair], axis=0)

        def rows_of(m):
            return slice(m * FINE, (m + 1) * FINE)

        def weave_rows(m):
            left = dot(tabs["weave_rows"][rows_of(m), :], state["quad", c])
            high, low = split(left[:, :coarse] + left[:, coarse:])
            state["a", c, m] = jnp.concatenate([high, low], axis=1)

        def slope_rows(m):
            light = dot(state.pop(("a", c, m)), tabs["weave_up"][...])
            light = light[:, :TS] + light[:, TS:]
            bend = jnp.tanh((0.5 * resist_gain) * light - 0.5 * resist_gain * resist_level)
            wanted = target_v[rows_of(m), c * TS : (c + 1) * TS]
            slope = ((0.25 * resist_gain) * (bend + 1.0) - (0.5 * resist_gain) * wanted) * (1.0 - bend * bend)
            state["g", c, m] = split(slope)

        def fold_rows(m):
            high, low = state.pop(("g", c, m))
            part = dot(high, tabs["weave_cols"][...]) + dot(low, tabs["weave_cols"][...])
            high, low = split(part[:, :coarse] + part[:, coarse:])
            woven[c, rows_of(m), :] = jnp.concatenate([high, low], axis=1)

        def finish():
            part = dot(tabs["weave_down"][...], woven[c])
            part = part[:coarse] + part[coarse:]
            pull = 2.0 * (part[:, :coarse] + part[:, coarse:])
            turned = pltpu.roll(pull, freqs, 1)
            state["pull", c] = jnp.concatenate(
                [jnp.where(first_half, pull, turned), jnp.where(first_half, turned, pull)], axis=1
            )

        stages = (weave_rows, slope_rows, fold_rows)
        count = TS // FINE
        middle = [
            functools.partial(stages[k], t - k)
            for t in range(count + 2) for k in (2, 1, 0) if 0 <= t - k < count
        ]
        return [begin] + middle + [finish]

    def fall(c, first, i):
        for k in (2 * i, 2 * i + 1):
            high, low = split(fields[c % plan.stores, first + k] * state["pull", c])
            sums = []
            for h in range(2):
                left = jnp.concatenate([lane_block(high, h), lane_block(low, h)], axis=1)
                part = dot(left, tabs["down_cols"][h])
                sums.append(part[:, :band] + part[:, band:])
            along = shift[1, first + k] + reach
            flip = jnp.where(residue >= along, 1.0, -1.0).astype(f32)
            high, low = split(sums[0] + flip * sums[1])
            lifts[c, :band, k * band : (k + 1) * band] = high
            lifts[c, band:, k * band : (k + 1) * band] = low

    def settle(c, first, i):
        part = dot(tabs["down_rows"][...], lifts[c, :, 2 * i * band : 2 * (i + 1) * band])
        part = part[:band] + part[band:]
        for k in range(2):
            s = first + 2 * i + k
            mine = lane_block(part, k)
            mine = (mine[:freqs] + sign * pltpu.roll(mine[freqs:], freqs, 1)) * pupils[s]
            rows = pl.ds(shift[0, s] + reach, freqs)
            close = residue >= shift[1, s] + reach
            zero = jnp.zeros_like(mine)
            grads[c, 0, rows, :] += jnp.where(close, mine, zero)
            grads[c, 1, rows, :] += jnp.where(close, zero, mine)

    def steps(stage, c, first=0):
        return [functools.partial(stage, c, first, i) for i in range(pairs)]

    grads[...] = jnp.zeros_like(grads)
    tiles = range(plan.tile_cols)
    rounds = sources // group
    if rounds == 1:
        for c in tiles:
            state["power", c] = jnp.zeros((coarse, 2 * coarse), f32)
        stages = [
            lambda c: [functools.partial(transform, c)],
            lambda c: steps(gather, c),
            lambda c: steps(lift, c),
            lambda c: steps(light_up, c),
            fine_steps,
            lambda c: steps(fall, c),
            lambda c: steps(settle, c),
        ]
        wants = {
            2: ("up_rows", "up_cols"),
            4: ("target", "weave_rows", "weave_up", "weave_cols", "weave_down"),
            5: ("down_rows", "down_cols"),
        }
        for t in range(len(stages) + LAG * (plan.tile_cols - 1)):
            need(*wants.get(t, ()))
            run(merged(*[stages[t - LAG * c](c) for c in tiles if 0 <= t - LAG * c < len(stages)]))
    else:
        need(*(name for name in names if not name.startswith("final")))
        for c in tiles:
            transform(c)

            def forward(g, power):
                state["power", c] = power
                for stage in (gather, lift, light_up):
                    run(steps(stage, c, g * group))
                return state["power", c]

            def backward(g, carry):
                for stage in (fall, settle):
                    run(steps(stage, c, g * group))
                return carry

            state["power", c] = lax.fori_loop(0, rounds, forward, jnp.zeros((coarse, 2 * coarse), f32))
            run(fine_steps(c))
            lax.fori_loop(0, rounds, backward, 0)

    need("final_cols", "final_rows")
    wide = plan.wide
    bands = jnp.concatenate([grads[c, k] for c in range(plan.tile_cols) for k in range(2)], axis=1)
    high, low = split(bands)
    part = dot(high, final_tab[...])
    part = part[:, : 2 * wide] + part[:, 2 * wide :] + dot(low, final_tab[:, : 2 * wide])
    high, low = split(jnp.concatenate([part[:, :wide], part[:, wide:]], axis=0))
    rows_high, rows_low = tabs["final_rows"][0], tabs["final_rows"][1]
    final = dot(rows_high, high) + dot(rows_high, low) + dot(rows_low, high)
    whole_grad[...] = final[:, : plan.width]
    rim_start = pl.multiple_of(jnp.where(tile_row == 0, HALO + TS, 0), HALO)
    ends = [
        pltpu.make_async_copy(whole_grad.at[pl.ds(rim_start, HALO)], row_out, sems.at[0]),
        pltpu.make_async_copy(whole_grad.at[pl.ds(HALO, TS)], own_out, sems.at[1]),
    ]
    for end in ends:
        end.start()
    for end in ends:
        end.wait()


def local_image(plan, mask, target, pupil, source_shift, source_weight, halo):
    tables = plan.tables()
    chunks = {f"mask{i}": mask for i in range(plan.cols // CHUNK)}
    arrays = {"pupil": pupil, "e_own": tables["e_own"], "e_rim": tables["e_rim"], "halo": halo}
    arrays.update(chunks)
    arrays.update((n, tables[n]) for n in ("cols", "up_rows", "up_cols", "weave_rows", "weave_up"))
    arrays["target"] = target
    arrays.update((n, t) for n, t in tables.items() if n not in arrays)
    names = tuple(arrays)
    picked = ("e_rim", "final_cols")
    local = {n: a.shape[1:] if n in picked else a.shape for n, a in arrays.items()}
    local.update({n: (TS, CHUNK) for n in chunks})
    smem = pl.BlockSpec(memory_space=pltpu.SMEM)
    distant = pl.BlockSpec(memory_space=pltpu.MemorySpace.HBM)
    sources, group, tile_cols = plan.sources, plan.group, plan.tile_cols
    band, coarse = plan.band, plan.coarse
    return pl.pallas_call(
        functools.partial(image_kernel, plan, names),
        out_shape=[
            jax.ShapeDtypeStruct((TS, plan.width), f32),
            jax.ShapeDtypeStruct((HALO, plan.width), f32),
        ],
        in_specs=[smem, smem] + [distant] * len(names),
        out_specs=[distant] * 2,
        scratch_shapes=[pltpu.VMEM(local[n], arrays[n].dtype) for n in names]
        + [
            pltpu.VMEM((sources, plan.freqs, band), f32),
            pltpu.VMEM((tile_cols, 4, band, band), f32),
            pltpu.VMEM((plan.stores, sources, coarse, 2 * coarse), f32),
            pltpu.VMEM((tile_cols, 2, band, band), f32),
            pltpu.VMEM((PAD, plan.width), f32),
            pltpu.VMEM((2 * band, plan.cols), bf16),
            pltpu.VMEM((2 * band, plan.cols), bf16),
            pltpu.VMEM((tile_cols, TS, 2 * coarse), bf16),
            pltpu.VMEM((tile_cols, 2 * band, group * band), bf16),
            pltpu.VMEM((tile_cols, group, coarse, 2 * band), bf16),
            pltpu.SemaphoreType.DMA((len(names),)),
        ],
        compiler_params=pltpu.CompilerParams(vmem_limit_bytes=60 * 1024 * 1024),
        name="image",
    )(source_shift.T, source_weight, *[jnp.asarray(arrays[n]) for n in names])


def shards(plan, mask, target, pupil, source_shift, source_weight):
    tile_row = lax.axis_index("tile")
    swap = [(0, 1), (1, 0)]
    edge = lax.dynamic_slice_in_dim(mask, jnp.where(tile_row == 0, TS - HALO, 0), HALO, 0)
    halo = lax.ppermute(edge, "tile", swap)
    own, row = local_image(plan, mask, target, pupil, source_shift, source_weight, halo)
    row = lax.ppermute(row, "tile", swap)
    first = jnp.where(tile_row == 0, TS - HALO, 0)
    return lax.dynamic_update_slice_in_dim(own, lax.dynamic_slice_in_dim(own, first, HALO, 0) + row, first, 0)


def solution(mesh):
    sizes = dict(mesh.shape)

    def run(mask, target, pupil, source_shift, source_weight):
        plan = Plan(pupil.shape[0], mask.shape[1], sizes["src"], source_shift.shape[0])
        placed = (P(("groups", "tile"), None), P(("groups", "tile"), None), P(), P(), P())
        return jax.shard_map(
            functools.partial(shards, plan),
            mesh=mesh,
            in_specs=placed,
            out_specs=P(("groups", "tile"), "src"),
            check_vma=False,
        )(mask, target, pupil, source_shift, source_weight)

    return run
```

```python
import functools
import math

import jax
import jax.numpy as jnp
import ml_dtypes
import numpy as np
from jax import lax
from jax.experimental import pallas as pl
from jax.experimental.pallas import tpu as pltpu
from jax.sharding import PartitionSpec as P

TS = 512
HALO = 64
PAD = TS + 2 * HALO
LANES = 128
FINE = 256
CHUNK = 512
LAG = 1
MOST = 24

resist_gain = 25.0
resist_level = 0.25

f32 = jnp.float32
bf16 = jnp.bfloat16


def halves(table):
    table = np.asarray(table, np.float64)
    high = table.astype(np.float32).astype(ml_dtypes.bfloat16)
    low = (table - high.astype(np.float64)).astype(np.float32).astype(ml_dtypes.bfloat16)
    return high, low


def turns(left, right, period):
    angle = 2.0 * np.pi * np.mod(np.outer(left, right), period) / period
    return np.cos(angle), np.sin(angle)


def both(table, axis):
    return np.concatenate(halves(table), axis=axis)


def split(value):
    high = value.astype(bf16)
    return high, (value - high.astype(f32)).astype(bf16)


def dot(left, right):
    return lax.dot_general(left, right, (((1,), (0,)), ((), ())), preferred_element_type=f32)


class Plan:
    def __init__(self, freqs, cols, n_src, sources):
        self.freqs = freqs
        self.reach = (3 * freqs) // 8
        self.band = 2 * freqs
        self.coarse = 2 * freqs
        self.cols = cols
        self.tile_cols = cols // TS
        self.width = cols // n_src
        self.wide = -(-self.width // LANES) * LANES
        self.n_src = n_src
        self.sources = sources
        self.group = max(n for n in range(2, MOST + 1, 2) if sources % n == 0)
        self.stores = self.tile_cols if sources <= MOST else 1
        self.spans = [
            (max(0, c * TS - LANES), min(cols, (c + 1) * TS + LANES)) for c in range(self.tile_cols)
        ]

    def tables(self):
        freqs, band, coarse = self.freqs, self.band, self.coarse
        index = np.arange(band)
        used = (index < freqs + 2 * self.reach).astype(np.float64)
        centre = index - (freqs // 2 + self.reach)
        out = {}
        cosine, sine = turns(centre, np.arange(PAD), PAD)
        rows = np.concatenate([cosine, -sine], axis=0) * np.concatenate([used, used])[:, None]
        out["e_own"] = both(rows[:, HALO : HALO + TS], 0)
        rims = []
        for rim in (rows[:, HALO + TS :], rows[:, :HALO]):
            high, low = halves(rim)
            rims.append(np.concatenate([high, low, high], axis=1))
        out["e_rim"] = np.stack(rims)

        def fold(real, imag):
            return np.concatenate(
                [real[:, :freqs], imag[:, :freqs], real[:, freqs:], imag[:, freqs:]], axis=1
            )

        place = np.arange(-LANES, TS + LANES) + HALO
        inside = ((place >= 0) & (place < PAD)).astype(np.float64)[:, None] * used
        cosine, sine = turns(place, centre, PAD)
        out["cols"] = both(fold(cosine * inside, -sine * inside), 1)
        relative = np.arange(freqs) - freqs // 2
        points = np.arange(coarse)
        cosine, sine = turns(points, relative, coarse)
        high, low = halves(np.concatenate([cosine, -sine], axis=1))
        out["up_rows"] = np.concatenate(
            [np.concatenate([high, high], axis=1), np.concatenate([low, low], axis=1)], axis=0
        )
        high, low = halves(np.concatenate([cosine.T, sine.T], axis=0))
        out["down_rows"] = np.concatenate(
            [np.concatenate([high, high], axis=1), np.concatenate([low, low], axis=1)], axis=0
        )
        order = np.concatenate([points[::2], points[1::2]])
        up, down = [], []
        for some in (points[::2], points[1::2]):
            cosine, sine = turns(centre[:freqs], some, coarse)
            table = np.concatenate(
                [np.concatenate([cosine, sine], axis=1), np.concatenate([-sine, cosine], axis=1)], axis=0
            )
            for into, piece in ((up, table), (down, table.T)):
                pair = both(piece, 1)
                into.append(np.concatenate([pair, pair], axis=0))
        out["up_cols"], out["down_cols"] = np.stack(up), np.stack(down)
        spread = (np.arange(TS) + HALO)[:, None] - (PAD // coarse) * points[None, :]
        weave = np.ones(spread.shape)
        for p in range(1, freqs):
            weave = weave + 2.0 * np.cos(2.0 * np.pi * np.mod(p * spread, PAD) / PAD)
        weave = weave / coarse
        out["weave_rows"] = both(weave, 1)
        out["weave_cols"] = both(weave[:, order], 1)
        turned = both(weave[:, order].T, 1)
        out["weave_up"] = np.concatenate([turned, turned], axis=0)
        out["weave_down"] = both(weave.T, 0)
        blocks = []
        for j in range(self.n_src):
            pieces = []
            for c in range(self.tile_cols):
                place = np.arange(j * self.width, (j + 1) * self.width) - c * TS + HALO
                inside = ((place >= 0) & (place < PAD)).astype(np.float64)[:, None] * used
                cosine = np.zeros((self.wide, band))
                sine = np.zeros((self.wide, band))
                cosine[: self.width], sine[: self.width] = turns(place, centre, PAD)
                cosine[: self.width] *= inside
                sine[: self.width] *= inside
                pieces.append(
                    np.concatenate([fold(cosine, -sine), fold(sine, cosine)], axis=0).T
                )
            blocks.append(both(np.concatenate(pieces, axis=0), 1))
        out["final_cols"] = np.stack(blocks)
        out["own_rows"] = np.stack(halves(rows.T[HALO : HALO + TS]))
        out["final_rows"] = np.stack([both(rows.T[HALO + TS :], 0), both(rows.T[:HALO], 0)])
        return {name: np.ascontiguousarray(value) for name, value in out.items()}


def merged(*lists):
    keyed = [((i + 0.5) / len(steps), n, step) for n, steps in enumerate(lists) for i, step in enumerate(steps)]
    return [step for _, _, step in sorted(keyed, key=lambda item: item[:2])]


def run(steps):
    for step in steps:
        step()


def image_kernel(plan, names, shift, weight, *refs):
    far = dict(zip(names, refs[: len(names)]))
    tail_out, row_out = refs[len(names) : len(names) + 2]
    near = dict(zip(names, refs[len(names) + 2 :]))
    (
        pupils, spectrum, fields, grads, tail, rim, u_high, u_low, woven, lifts, lines, sems,
    ) = refs[2 * len(names) + 2 :]
    sources, group = plan.sources, plan.group
    freqs, reach, band, coarse = plan.freqs, plan.reach, plan.band, plan.coarse
    tile_row = lax.axis_index("tile")
    block = lax.axis_index("src")
    picked = {"e_rim": tile_row, "final_cols": block, "final_rows": tile_row}
    pending = {}
    spans = {f"mask{n}": slice(n, n + CHUNK) for n in range(0, plan.cols, CHUNK)}
    for i, name in enumerate(names):
        source = far[name].at[picked[name]] if name in picked else far[name]
        if name in spans:
            source = source.at[:, spans[name]]
        pending[name] = pltpu.make_async_copy(source, near[name], sems.at[i])
    early = [name for name in names if name in ("pupil", "e_own", "e_rim", "halo", "cols") or name in spans]
    for name in early:
        pending[name].start()

    def need(*wanted):
        for name in wanted:
            if name in pending:
                pending.pop(name).wait()

    tabs = near
    target_v, e_rim, final_tab, halo = (
        near[name] for name in ("target", "e_rim", "final_cols", "halo")
    )
    total = weight[0]
    for s in range(1, sources):
        total = total + weight[s]
    scale = 1.0 / (PAD * PAD)
    lane = lax.broadcasted_iota(jnp.int32, (1, band), 1)
    first_half = lane < freqs
    residue = jnp.where(first_half, lane, lane - freqs)
    sign = jnp.where(first_half, 1.0, -1.0).astype(f32)
    need("pupil")
    doubled = jnp.concatenate([near["pupil"][...]] * 2, axis=1)

    def place_pupil(s):
        strength = jnp.sqrt(jnp.full((1, band), weight[s] / total, f32)) * scale
        pupils[s] = pltpu.roll(doubled, shift[1, s] + reach, 1) * strength

    if sources <= MOST:
        for s in range(sources):
            place_pupil(s)
    else:
        lax.fori_loop(0, sources, lambda s, c: (place_pupil(s), c)[1], 0)

    need("e_own", "e_rim", "halo")
    for name, cols in spans.items():
        need(name)
        if cols.start == 0:
            for late in names:
                if late not in early:
                    pending[late].start()
        rim_high, rim_low = split(halo[:, cols])
        rows = dot(e_rim[...], jnp.concatenate([rim_high, rim_high, rim_low], axis=0))
        high, low = split(near[name][...])
        part = dot(near["e_own"][...], high)
        rows = rows + part[: 2 * band] + part[2 * band :] + dot(near["e_own"][: 2 * band, :], low)
        high, low = split(rows)
        u_high[:, cols] = high
        u_low[:, cols] = low
    need("cols")

    def transform(c):
        first, last = plan.spans[c]
        inside = slice(first - c * TS + LANES, last - c * TS + LANES)
        prod = dot(u_high[:, first:last], tabs["cols"][inside, :])
        prod = prod[:, : 2 * band] + prod[:, 2 * band :]
        prod = prod + dot(u_low[:, first:last], tabs["cols"][inside, : 2 * band])
        for k in range(2):
            own, other = prod[:band, k * band : (k + 1) * band], prod[band:, k * band : (k + 1) * band]
            half = own - sign * pltpu.roll(other, freqs, 1)
            spectrum[c, k] = half
            spectrum[c, 2 + k] = pltpu.roll(half, freqs, 1) * sign

    def lane_block(value, k):
        return value[:, k * band : (k + 1) * band]

    pairs = group // 2
    state = {}

    def gather(c, first, i):
        for k in (2 * i, 2 * i + 1):
            down = shift[0, first + k] + reach
            along = shift[1, first + k] + reach
            rows = pl.ds(down, freqs)
            close = residue >= along
            upper = jnp.where(close, spectrum[c, 0, rows, :], spectrum[c, 1, rows, :])
            lower = jnp.where(close, spectrum[c, 2, rows, :], spectrum[c, 3, rows, :])
            scaled = pupils[first + k]
            high, low = split(jnp.concatenate([upper * scaled, lower * scaled], axis=0))
            lifts[c, :band, k * band : (k + 1) * band] = high
            lifts[c, band:, k * band : (k + 1) * band] = low

    def lift(c, first, i):
        lifted = dot(tabs["up_rows"][...], lifts[c, :, 2 * i * band : 2 * (i + 1) * band])
        high, low = split(lifted[:coarse] + lifted[coarse:])
        for k in range(2):
            lines[c, 2 * i + k, :, :band] = lane_block(high, k)
            lines[c, 2 * i + k, :, band:] = lane_block(low, k)

    def light_up(c, first, i):
        for k in (2 * i, 2 * i + 1):
            along = shift[1, first + k] + reach
            flip = jnp.where(residue >= along, 1.0, -1.0).astype(bf16)
            line = lines[c, k]
            even = dot(line, tabs["up_cols"][0])
            odd = dot(line * jnp.concatenate([flip, flip], axis=1), tabs["up_cols"][1])
            field = jnp.concatenate(
                [even[:, :coarse] + even[:, coarse:], odd[:, :coarse] + odd[:, coarse:]], axis=1
            )
            fields[c % plan.stores, first + k] = field
            state["power", c] = state["power", c] + field * field

    def fine_steps(c):
        def begin():
            power = state.pop(("power", c))
            even, odd = power[:, :coarse], power[:, coarse:]
            power = jnp.where(first_half, even + pltpu.roll(even, freqs, 1), odd + pltpu.roll(odd, freqs, 1))
            high, low = split(power)
            pair = jnp.concatenate([high, low], axis=1)
            state["quad", c] = jnp.concatenate([pair, pair], axis=0)

        def rows_of(m):
            return slice(m * FINE, (m + 1) * FINE)

        def weave_rows(m):
            left = dot(tabs["weave_rows"][rows_of(m), :], state["quad", c])
            high, low = split(left[:, :coarse] + left[:, coarse:])
            state["a", c, m] = jnp.concatenate([high, low], axis=1)

        def slope_rows(m):
            light = dot(state.pop(("a", c, m)), tabs["weave_up"][...])
            light = light[:, :TS] + light[:, TS:]
            bend = jnp.tanh((0.5 * resist_gain) * light - 0.5 * resist_gain * resist_level)
            wanted = target_v[rows_of(m), c * TS : (c + 1) * TS]
            slope = ((0.25 * resist_gain) * (bend + 1.0) - (0.5 * resist_gain) * wanted) * (1.0 - bend * bend)
            state["g", c, m] = split(slope)

        def fold_rows(m):
            high, low = state.pop(("g", c, m))
            part = dot(high, tabs["weave_cols"][...]) + dot(low, tabs["weave_cols"][...])
            high, low = split(part[:, :coarse] + part[:, coarse:])
            woven[c, rows_of(m), :] = jnp.concatenate([high, low], axis=1)

        def finish():
            part = dot(tabs["weave_down"][...], woven[c])
            part = part[:coarse] + part[coarse:]
            pull = 2.0 * (part[:, :coarse] + part[:, coarse:])
            turned = pltpu.roll(pull, freqs, 1)
            state["pull", c] = jnp.concatenate(
                [jnp.where(first_half, pull, turned), jnp.where(first_half, turned, pull)], axis=1
            )

        stages = (weave_rows, slope_rows, fold_rows)
        count = TS // FINE
        middle = [
            functools.partial(stages[k], t - k)
            for t in range(count + 2) for k in (2, 1, 0) if 0 <= t - k < count
        ]
        return [begin] + middle + [finish]

    def fall(c, first, i):
        for k in (2 * i, 2 * i + 1):
            high, low = split(fields[c % plan.stores, first + k] * state["pull", c])
            sums = []
            for h in range(2):
                left = jnp.concatenate([lane_block(high, h), lane_block(low, h)], axis=1)
                part = dot(left, tabs["down_cols"][h])
                sums.append(part[:, :band] + part[:, band:])
            along = shift[1, first + k] + reach
            flip = jnp.where(residue >= along, 1.0, -1.0).astype(f32)
            high, low = split(sums[0] + flip * sums[1])
            lifts[c, :band, k * band : (k + 1) * band] = high
            lifts[c, band:, k * band : (k + 1) * band] = low

    def settle(c, first, i):
        part = dot(tabs["down_rows"][...], lifts[c, :, 2 * i * band : 2 * (i + 1) * band])
        part = part[:band] + part[band:]
        for k in range(2):
            s = first + 2 * i + k
            mine = lane_block(part, k)
            mine = (mine[:freqs] + sign * pltpu.roll(mine[freqs:], freqs, 1)) * pupils[s]
            rows = pl.ds(shift[0, s] + reach, freqs)
            close = residue >= shift[1, s] + reach
            zero = jnp.zeros_like(mine)
            grads[c, 0, rows, :] += jnp.where(close, mine, zero)
            grads[c, 1, rows, :] += jnp.where(close, zero, mine)

    def steps(stage, c, first=0):
        return [functools.partial(stage, c, first, i) for i in range(pairs)]

    grads[...] = jnp.zeros_like(grads)
    tiles = range(plan.tile_cols)
    rounds = sources // group
    if rounds == 1:
        for c in tiles:
            state["power", c] = jnp.zeros((coarse, 2 * coarse), f32)
        stages = [
            lambda c: [functools.partial(transform, c)],
            lambda c: steps(gather, c),
            lambda c: steps(lift, c),
            lambda c: steps(light_up, c),
            fine_steps,
            lambda c: steps(fall, c),
            lambda c: steps(settle, c),
        ]
        wants = {
            2: ("up_rows", "up_cols"),
            4: ("target", "weave_rows", "weave_up", "weave_cols", "weave_down"),
            5: ("down_rows", "down_cols"),
        }
        for t in range(len(stages) + LAG * (plan.tile_cols - 1)):
            need(*wants.get(t, ()))
            run(merged(*[stages[t - LAG * c](c) for c in tiles if 0 <= t - LAG * c < len(stages)]))
    else:
        need(*(name for name in names if not name.startswith("final")))
        for c in tiles:
            transform(c)

            def forward(g, power):
                state["power", c] = power
                for stage in (gather, lift, light_up):
                    run(steps(stage, c, g * group))
                return state["power", c]

            def backward(g, carry):
                for stage in (fall, settle):
                    run(steps(stage, c, g * group))
                return carry

            state["power", c] = lax.fori_loop(0, rounds, forward, jnp.zeros((coarse, 2 * coarse), f32))
            run(fine_steps(c))
            lax.fori_loop(0, rounds, backward, 0)

    need("final_cols", "final_rows")
    wide = plan.wide
    bands = jnp.concatenate([grads[c, k] for c in range(plan.tile_cols) for k in range(2)], axis=1)
    high, low = split(bands)
    part = dot(high, final_tab[...])
    part = part[:, : 2 * wide] + part[:, 2 * wide :] + dot(low, final_tab[:, : 2 * wide])
    column_part = jnp.concatenate([part[:, :wide], part[:, wide:]], axis=0)
    tail[...] = column_part
    ends = [pltpu.make_async_copy(tail, tail_out, sems.at[0]), pltpu.make_async_copy(rim, row_out, sems.at[1])]
    ends[0].start()
    high, low = split(column_part)
    table = near["final_rows"]
    part = dot(table[...], high)
    part = part[:HALO] + part[HALO:] + dot(table[:HALO, :], low)
    rim[...] = part[:, : plan.width]
    ends[1].start()
    for end in ends:
        end.wait()


def own_kernel(plan, tail, table, out):
    high, low = split(tail[...])
    part = dot(table[0], high) + dot(table[0], low) + dot(table[1], high)
    out[...] = part[:, : plan.width]


def add_kernel(own, row, out):
    tile_row = lax.axis_index("tile")
    out[...] = own[...]
    first = pl.multiple_of(jnp.where(tile_row == 0, TS - HALO, 0), HALO)
    out[pl.ds(first, HALO), :] = own[pl.ds(first, HALO), :] + row[...]


def own_rows(plan, tables, tail):
    vmem = pl.BlockSpec(memory_space=pltpu.VMEM)
    return pl.pallas_call(
        functools.partial(own_kernel, plan),
        out_shape=jax.ShapeDtypeStruct((TS, plan.width), f32),
        in_specs=[vmem] * 2,
        out_specs=vmem,
        compiler_params=pltpu.CompilerParams(vmem_limit_bytes=8 * 1024 * 1024),
        cost_estimate=pl.CostEstimate(flops=10**9, bytes_accessed=10**6, transcendentals=0),
        name="own_rows",
    )(tail, jnp.asarray(tables["own_rows"]))


def local_image(plan, tables, mask, target, pupil, source_shift, source_weight, halo):
    arrays = {"pupil": pupil, "e_own": tables["e_own"], "e_rim": tables["e_rim"], "halo": halo}
    arrays.update((f"mask{n}", mask) for n in range(0, plan.cols, CHUNK))
    arrays.update((n, tables[n]) for n in ("cols", "up_rows", "up_cols", "weave_rows", "weave_up"))
    arrays["target"] = target
    arrays.update((n, t) for n, t in tables.items() if n not in arrays and n != "own_rows")
    names = tuple(arrays)
    picked = ("e_rim", "final_cols", "final_rows")
    local = {n: a.shape[1:] if n in picked else a.shape for n, a in arrays.items()}
    local.update((n, (TS, CHUNK)) for n in names if n.startswith("mask"))
    smem = pl.BlockSpec(memory_space=pltpu.SMEM)
    distant = pl.BlockSpec(memory_space=pltpu.MemorySpace.HBM)
    sources, group, tile_cols = plan.sources, plan.group, plan.tile_cols
    band, coarse = plan.band, plan.coarse
    return pl.pallas_call(
        functools.partial(image_kernel, plan, names),
        out_shape=[
            jax.ShapeDtypeStruct((2 * band, plan.wide), f32),
            jax.ShapeDtypeStruct((HALO, plan.width), f32),
        ],
        in_specs=[smem, smem] + [distant] * len(names),
        out_specs=[distant] * 2,
        scratch_shapes=[pltpu.VMEM(local[n], arrays[n].dtype) for n in names]
        + [
            pltpu.VMEM((sources, plan.freqs, band), f32),
            pltpu.VMEM((tile_cols, 4, band, band), f32),
            pltpu.VMEM((plan.stores, sources, coarse, 2 * coarse), f32),
            pltpu.VMEM((tile_cols, 2, band, band), f32),
            pltpu.VMEM((2 * band, plan.wide), f32),
            pltpu.VMEM((HALO, plan.width), f32),
            pltpu.VMEM((2 * band, plan.cols), bf16),
            pltpu.VMEM((2 * band, plan.cols), bf16),
            pltpu.VMEM((tile_cols, TS, 2 * coarse), bf16),
            pltpu.VMEM((tile_cols, 2 * band, group * band), bf16),
            pltpu.VMEM((tile_cols, group, coarse, 2 * band), bf16),
            pltpu.SemaphoreType.DMA((len(names),)),
        ],
        compiler_params=pltpu.CompilerParams(vmem_limit_bytes=60 * 1024 * 1024),
        name="image",
    )(source_shift.T, source_weight, *[jnp.asarray(arrays[n]) for n in names])


def shards(plan, mask, target, pupil, source_shift, source_weight):
    tile_row = lax.axis_index("tile")
    swap = [(0, 1), (1, 0)]
    edge = lax.dynamic_slice_in_dim(mask, jnp.where(tile_row == 0, TS - HALO, 0), HALO, 0)
    halo = lax.ppermute(edge, "tile", swap)
    tables = plan.tables()
    tail, row = local_image(plan, tables, mask, target, pupil, source_shift, source_weight, halo)
    row = lax.ppermute(row, "tile", swap)
    own = own_rows(plan, tables, tail)
    vmem = pl.BlockSpec(memory_space=pltpu.VMEM)
    return pl.pallas_call(
        add_kernel,
        out_shape=jax.ShapeDtypeStruct((TS, plan.width), f32),
        in_specs=[vmem] * 2,
        out_specs=vmem,
        compiler_params=pltpu.CompilerParams(vmem_limit_bytes=8 * 1024 * 1024),
        name="add_rows",
    )(own, row)


def solution(mesh):
    sizes = dict(mesh.shape)

    def run(mask, target, pupil, source_shift, source_weight):
        plan = Plan(pupil.shape[0], mask.shape[1], sizes["src"], source_shift.shape[0])
        placed = (P(("groups", "tile"), None), P(("groups", "tile"), None), P(), P(), P())
        return jax.shard_map(
            functools.partial(shards, plan),
            mesh=mesh,
            in_specs=placed,
            out_specs=P(("groups", "tile"), "src"),
            check_vma=False,
        )(mask, target, pupil, source_shift, source_weight)

    return run
```

```python
import functools
import math

import jax
import jax.numpy as jnp
import ml_dtypes
import numpy as np
from jax import lax
from jax.experimental import pallas as pl
from jax.experimental.pallas import tpu as pltpu
from jax.sharding import PartitionSpec as P

TS = 512
HALO = 64
PAD = TS + 2 * HALO
LANES = 128
FINE = 256
CHUNK = 512
LAG = 1
MOST = 24

resist_gain = 25.0
resist_level = 0.25

f32 = jnp.float32
bf16 = jnp.bfloat16


def halves(table):
    table = np.asarray(table, np.float64)
    high = table.astype(np.float32).astype(ml_dtypes.bfloat16)
    low = (table - high.astype(np.float64)).astype(np.float32).astype(ml_dtypes.bfloat16)
    return high, low


def turns(left, right, period):
    angle = 2.0 * np.pi * np.mod(np.outer(left, right), period) / period
    return np.cos(angle), np.sin(angle)


def both(table, axis):
    return np.concatenate(halves(table), axis=axis)


def split(value):
    high = value.astype(bf16)
    return high, (value - high.astype(f32)).astype(bf16)


def dot(left, right):
    return lax.dot_general(left, right, (((1,), (0,)), ((), ())), preferred_element_type=f32)


class Plan:
    def __init__(self, freqs, cols, n_src, sources):
        self.freqs = freqs
        self.reach = (3 * freqs) // 8
        self.band = 2 * freqs
        self.coarse = 2 * freqs
        self.cols = cols
        self.tile_cols = cols // TS
        self.width = cols // n_src
        self.wide = -(-self.width // LANES) * LANES
        self.n_src = n_src
        self.sources = sources
        self.group = max(n for n in range(2, MOST + 1, 2) if sources % n == 0)
        self.stores = self.tile_cols if sources <= MOST else 1
        self.spans = [
            (max(0, c * TS - LANES), min(cols, (c + 1) * TS + LANES)) for c in range(self.tile_cols)
        ]

    def tables(self):
        freqs, band, coarse = self.freqs, self.band, self.coarse
        index = np.arange(band)
        used = (index < freqs + 2 * self.reach).astype(np.float64)
        centre = index - (freqs // 2 + self.reach)
        out = {}
        cosine, sine = turns(centre, np.arange(PAD), PAD)
        rows = np.concatenate([cosine, -sine], axis=0) * np.concatenate([used, used])[:, None]
        out["e_own"] = both(rows[:, HALO : HALO + TS], 0)
        rims = []
        for rim in (rows[:, HALO + TS :], rows[:, :HALO]):
            high, low = halves(rim)
            rims.append(np.concatenate([high, low, high], axis=1))
        out["e_rim"] = np.stack(rims)

        def fold(real, imag):
            return np.concatenate(
                [real[:, :freqs], imag[:, :freqs], real[:, freqs:], imag[:, freqs:]], axis=1
            )

        place = np.arange(-LANES, TS + LANES) + HALO
        inside = ((place >= 0) & (place < PAD)).astype(np.float64)[:, None] * used
        cosine, sine = turns(place, centre, PAD)
        out["cols"] = both(fold(cosine * inside, -sine * inside), 1)
        relative = np.arange(freqs) - freqs // 2
        points = np.arange(coarse)
        cosine, sine = turns(points, relative, coarse)
        high, low = halves(np.concatenate([cosine, -sine], axis=1))
        out["up_rows"] = np.concatenate(
            [np.concatenate([high, high], axis=1), np.concatenate([low, low], axis=1)], axis=0
        )
        high, low = halves(np.concatenate([cosine.T, sine.T], axis=0))
        out["down_rows"] = np.concatenate(
            [np.concatenate([high, high], axis=1), np.concatenate([low, low], axis=1)], axis=0
        )
        order = np.concatenate([points[::2], points[1::2]])
        up, down = [], []
        for some in (points[::2], points[1::2]):
            cosine, sine = turns(centre[:freqs], some, coarse)
            table = np.concatenate(
                [np.concatenate([cosine, sine], axis=1), np.concatenate([-sine, cosine], axis=1)], axis=0
            )
            for into, piece in ((up, table), (down, table.T)):
                pair = both(piece, 1)
                into.append(np.concatenate([pair, pair], axis=0))
        out["up_cols"], out["down_cols"] = np.stack(up), np.stack(down)
        spread = (np.arange(TS) + HALO)[:, None] - (PAD // coarse) * points[None, :]
        weave = np.ones(spread.shape)
        for p in range(1, freqs):
            weave = weave + 2.0 * np.cos(2.0 * np.pi * np.mod(p * spread, PAD) / PAD)
        weave = weave / coarse
        out["weave_rows"] = both(weave, 1)
        out["weave_cols"] = both(weave[:, order], 1)
        turned = both(weave[:, order].T, 1)
        out["weave_up"] = np.concatenate([turned, turned], axis=0)
        out["weave_down"] = both(weave.T, 0)
        blocks = []
        for j in range(self.n_src):
            pieces = []
            for c in range(self.tile_cols):
                place = np.arange(j * self.width, (j + 1) * self.width) - c * TS + HALO
                inside = ((place >= 0) & (place < PAD)).astype(np.float64)[:, None] * used
                cosine = np.zeros((self.wide, band))
                sine = np.zeros((self.wide, band))
                cosine[: self.width], sine[: self.width] = turns(place, centre, PAD)
                cosine[: self.width] *= inside
                sine[: self.width] *= inside
                pieces.append(
                    np.concatenate([fold(cosine, -sine), fold(sine, cosine)], axis=0).T
                )
            blocks.append(both(np.concatenate(pieces, axis=0), 1))
        out["final_cols"] = np.stack(blocks)
        out["own_rows"] = np.stack(halves(rows.T[HALO : HALO + TS]))
        out["final_rows"] = np.stack([both(rows.T[HALO + TS :], 0), both(rows.T[:HALO], 0)])
        return {name: np.ascontiguousarray(value) for name, value in out.items()}


def merged(*lists):
    keyed = [((i + 0.5) / len(steps), n, step) for n, steps in enumerate(lists) for i, step in enumerate(steps)]
    return [step for _, _, step in sorted(keyed, key=lambda item: item[:2])]


def run(steps):
    for step in steps:
        step()


def image_kernel(plan, names, shift_far, weight_far, *refs):
    far = dict(zip(names, refs[: len(names)]))
    tail_out, row_out = refs[len(names) : len(names) + 2]
    near = dict(zip(names, refs[len(names) + 2 :]))
    (
        pupils, spectrum, fields, grads, tail, rim, u_high, u_low, woven, lifts, lines, shift, weight, sems,
    ) = refs[2 * len(names) + 2 :]
    sources, group = plan.sources, plan.group
    freqs, reach, band, coarse = plan.freqs, plan.reach, plan.band, plan.coarse
    tile_row = lax.axis_index("tile")
    block = lax.axis_index("src")
    picked = {"e_rim": tile_row, "final_cols": block, "final_rows": tile_row}
    scalars = [
        pltpu.make_async_copy(shift_far, shift, sems.at[len(names)]),
        pltpu.make_async_copy(weight_far, weight, sems.at[len(names) + 1]),
    ]
    for copy in scalars:
        copy.start()
    pending = {}
    spans = {f"mask{n}": slice(n, n + CHUNK) for n in range(0, plan.cols, CHUNK)}
    for i, name in enumerate(names):
        source = far[name].at[picked[name]] if name in picked else far[name]
        if name in spans:
            source = source.at[:, spans[name]]
        pending[name] = pltpu.make_async_copy(source, near[name], sems.at[i])
    early = [name for name in names if name in ("pupil", "e_own", "e_rim", "halo", "cols") or name in spans]
    for name in early:
        pending[name].start()

    def need(*wanted):
        for name in wanted:
            if name in pending:
                pending.pop(name).wait()

    tabs = near
    target_v, e_rim, final_tab, halo = (
        near[name] for name in ("target", "e_rim", "final_cols", "halo")
    )
    for copy in scalars:
        copy.wait()
    total = weight[0]
    for s in range(1, sources):
        total = total + weight[s]
    scale = 1.0 / (PAD * PAD)
    lane = lax.broadcasted_iota(jnp.int32, (1, band), 1)
    first_half = lane < freqs
    residue = jnp.where(first_half, lane, lane - freqs)
    sign = jnp.where(first_half, 1.0, -1.0).astype(f32)
    need("pupil")
    doubled = jnp.concatenate([near["pupil"][...]] * 2, axis=1)

    def place_pupil(s):
        strength = jnp.sqrt(jnp.full((1, band), weight[s] / total, f32)) * scale
        pupils[s] = pltpu.roll(doubled, shift[1, s] + reach, 1) * strength

    if sources <= MOST:
        for s in range(sources):
            place_pupil(s)
    else:
        lax.fori_loop(0, sources, lambda s, c: (place_pupil(s), c)[1], 0)

    need("e_own", "e_rim", "halo")
    for name, cols in spans.items():
        need(name)
        if cols.start == 0:
            for late in names:
                if late not in early:
                    pending[late].start()
        rim_high, rim_low = split(halo[:, cols])
        rows = dot(e_rim[...], jnp.concatenate([rim_high, rim_high, rim_low], axis=0))
        high, low = split(near[name][...])
        part = dot(near["e_own"][...], high)
        rows = rows + part[: 2 * band] + part[2 * band :] + dot(near["e_own"][: 2 * band, :], low)
        high, low = split(rows)
        u_high[:, cols] = high
        u_low[:, cols] = low
    need("cols")

    def transform(c):
        first, last = plan.spans[c]
        inside = slice(first - c * TS + LANES, last - c * TS + LANES)
        prod = dot(u_high[:, first:last], tabs["cols"][inside, :])
        prod = prod[:, : 2 * band] + prod[:, 2 * band :]
        prod = prod + dot(u_low[:, first:last], tabs["cols"][inside, : 2 * band])
        for k in range(2):
            own, other = prod[:band, k * band : (k + 1) * band], prod[band:, k * band : (k + 1) * band]
            half = own - sign * pltpu.roll(other, freqs, 1)
            spectrum[c, k] = half
            spectrum[c, 2 + k] = pltpu.roll(half, freqs, 1) * sign

    def lane_block(value, k):
        return value[:, k * band : (k + 1) * band]

    pairs = group // 2
    state = {}

    def gather(c, first, i):
        for k in (2 * i, 2 * i + 1):
            down = shift[0, first + k] + reach
            along = shift[1, first + k] + reach
            rows = pl.ds(down, freqs)
            close = residue >= along
            upper = jnp.where(close, spectrum[c, 0, rows, :], spectrum[c, 1, rows, :])
            lower = jnp.where(close, spectrum[c, 2, rows, :], spectrum[c, 3, rows, :])
            scaled = pupils[first + k]
            high, low = split(jnp.concatenate([upper * scaled, lower * scaled], axis=0))
            lifts[c, :band, k * band : (k + 1) * band] = high
            lifts[c, band:, k * band : (k + 1) * band] = low

    def lift(c, first, i):
        lifted = dot(tabs["up_rows"][...], lifts[c, :, 2 * i * band : 2 * (i + 1) * band])
        high, low = split(lifted[:coarse] + lifted[coarse:])
        for k in range(2):
            lines[c, 2 * i + k, :, :band] = lane_block(high, k)
            lines[c, 2 * i + k, :, band:] = lane_block(low, k)

    def light_up(c, first, i):
        for k in (2 * i, 2 * i + 1):
            along = shift[1, first + k] + reach
            flip = jnp.where(residue >= along, 1.0, -1.0).astype(bf16)
            line = lines[c, k]
            even = dot(line, tabs["up_cols"][0])
            odd = dot(line * jnp.concatenate([flip, flip], axis=1), tabs["up_cols"][1])
            field = jnp.concatenate(
                [even[:, :coarse] + even[:, coarse:], odd[:, :coarse] + odd[:, coarse:]], axis=1
            )
            fields[c % plan.stores, first + k] = field
            state["power", c] = state["power", c] + field * field

    def fine_steps(c):
        def begin():
            power = state.pop(("power", c))
            even, odd = power[:, :coarse], power[:, coarse:]
            power = jnp.where(first_half, even + pltpu.roll(even, freqs, 1), odd + pltpu.roll(odd, freqs, 1))
            high, low = split(power)
            pair = jnp.concatenate([high, low], axis=1)
            state["quad", c] = jnp.concatenate([pair, pair], axis=0)

        def rows_of(m):
            return slice(m * FINE, (m + 1) * FINE)

        def weave_rows(m):
            left = dot(tabs["weave_rows"][rows_of(m), :], state["quad", c])
            high, low = split(left[:, :coarse] + left[:, coarse:])
            state["a", c, m] = jnp.concatenate([high, low], axis=1)

        def slope_rows(m):
            light = dot(state.pop(("a", c, m)), tabs["weave_up"][...])
            light = light[:, :TS] + light[:, TS:]
            bend = jnp.tanh((0.5 * resist_gain) * light - 0.5 * resist_gain * resist_level)
            wanted = target_v[rows_of(m), c * TS : (c + 1) * TS]
            slope = ((0.25 * resist_gain) * (bend + 1.0) - (0.5 * resist_gain) * wanted) * (1.0 - bend * bend)
            state["g", c, m] = split(slope)

        def fold_rows(m):
            high, low = state.pop(("g", c, m))
            part = dot(high, tabs["weave_cols"][...]) + dot(low, tabs["weave_cols"][...])
            high, low = split(part[:, :coarse] + part[:, coarse:])
            woven[c, rows_of(m), :] = jnp.concatenate([high, low], axis=1)

        def finish():
            part = dot(tabs["weave_down"][...], woven[c])
            part = part[:coarse] + part[coarse:]
            pull = 2.0 * (part[:, :coarse] + part[:, coarse:])
            turned = pltpu.roll(pull, freqs, 1)
            state["pull", c] = jnp.concatenate(
                [jnp.where(first_half, pull, turned), jnp.where(first_half, turned, pull)], axis=1
            )

        stages = (weave_rows, slope_rows, fold_rows)
        count = TS // FINE
        middle = [
            functools.partial(stages[k], t - k)
            for t in range(count + 2) for k in (2, 1, 0) if 0 <= t - k < count
        ]
        return [begin] + middle + [finish]

    def fall(c, first, i):
        for k in (2 * i, 2 * i + 1):
            high, low = split(fields[c % plan.stores, first + k] * state["pull", c])
            sums = []
            for h in range(2):
                left = jnp.concatenate([lane_block(high, h), lane_block(low, h)], axis=1)
                part = dot(left, tabs["down_cols"][h])
                sums.append(part[:, :band] + part[:, band:])
            along = shift[1, first + k] + reach
            flip = jnp.where(residue >= along, 1.0, -1.0).astype(f32)
            high, low = split(sums[0] + flip * sums[1])
            lifts[c, :band, k * band : (k + 1) * band] = high
            lifts[c, band:, k * band : (k + 1) * band] = low

    def settle(c, first, i):
        part = dot(tabs["down_rows"][...], lifts[c, :, 2 * i * band : 2 * (i + 1) * band])
        part = part[:band] + part[band:]
        for k in range(2):
            s = first + 2 * i + k
            mine = lane_block(part, k)
            mine = (mine[:freqs] + sign * pltpu.roll(mine[freqs:], freqs, 1)) * pupils[s]
            rows = pl.ds(shift[0, s] + reach, freqs)
            close = residue >= shift[1, s] + reach
            zero = jnp.zeros_like(mine)
            grads[c, 0, rows, :] += jnp.where(close, mine, zero)
            grads[c, 1, rows, :] += jnp.where(close, zero, mine)

    def steps(stage, c, first=0):
        return [functools.partial(stage, c, first, i) for i in range(pairs)]

    grads[...] = jnp.zeros_like(grads)
    tiles = range(plan.tile_cols)
    rounds = sources // group
    if rounds == 1:
        for c in tiles:
            state["power", c] = jnp.zeros((coarse, 2 * coarse), f32)
        stages = [
            lambda c: [functools.partial(transform, c)],
            lambda c: steps(gather, c),
            lambda c: steps(lift, c),
            lambda c: steps(light_up, c),
            fine_steps,
            lambda c: steps(fall, c),
            lambda c: steps(settle, c),
        ]
        wants = {
            2: ("up_rows", "up_cols"),
            4: ("target", "weave_rows", "weave_up", "weave_cols", "weave_down"),
            5: ("down_rows", "down_cols"),
        }
        for t in range(len(stages) + LAG * (plan.tile_cols - 1)):
            need(*wants.get(t, ()))
            run(merged(*[stages[t - LAG * c](c) for c in tiles if 0 <= t - LAG * c < len(stages)]))
    else:
        need(*(name for name in names if not name.startswith("final")))
        for c in tiles:
            transform(c)

            def forward(g, power):
                state["power", c] = power
                for stage in (gather, lift, light_up):
                    run(steps(stage, c, g * group))
                return state["power", c]

            def backward(g, carry):
                for stage in (fall, settle):
                    run(steps(stage, c, g * group))
                return carry

            state["power", c] = lax.fori_loop(0, rounds, forward, jnp.zeros((coarse, 2 * coarse), f32))
            run(fine_steps(c))
            lax.fori_loop(0, rounds, backward, 0)

    need("final_cols", "final_rows")
    wide = plan.wide
    bands = jnp.concatenate([grads[c, k] for c in range(plan.tile_cols) for k in range(2)], axis=1)
    high, low = split(bands)
    part = dot(high, final_tab[...])
    part = part[:, : 2 * wide] + part[:, 2 * wide :] + dot(low, final_tab[:, : 2 * wide])
    column_part = jnp.concatenate([part[:, :wide], part[:, wide:]], axis=0)
    tail[...] = column_part
    ends = [pltpu.make_async_copy(tail, tail_out, sems.at[0]), pltpu.make_async_copy(rim, row_out, sems.at[1])]
    ends[0].start()
    high, low = split(column_part)
    table = near["final_rows"]
    part = dot(table[...], high)
    part = part[:HALO] + part[HALO:] + dot(table[:HALO, :], low)
    rim[...] = part[:, : plan.width]
    ends[1].start()
    for end in ends:
        end.wait()


def own_kernel(plan, tail, table, out):
    high, low = split(tail[...])
    part = dot(table[0], high) + dot(table[0], low) + dot(table[1], high)
    out[...] = part[:, : plan.width]


def add_kernel(own, row, out):
    tile_row = lax.axis_index("tile")
    out[...] = own[...]
    first = pl.multiple_of(jnp.where(tile_row == 0, TS - HALO, 0), HALO)
    out[pl.ds(first, HALO), :] = own[pl.ds(first, HALO), :] + row[...]


def own_rows(plan, tables, tail):
    vmem = pl.BlockSpec(memory_space=pltpu.VMEM)
    return pl.pallas_call(
        functools.partial(own_kernel, plan),
        out_shape=jax.ShapeDtypeStruct((TS, plan.width), f32),
        in_specs=[vmem] * 2,
        out_specs=vmem,
        compiler_params=pltpu.CompilerParams(vmem_limit_bytes=8 * 1024 * 1024),
        cost_estimate=pl.CostEstimate(flops=10**9, bytes_accessed=10**6, transcendentals=0),
        name="own_rows",
    )(tail, jnp.asarray(tables["own_rows"]))


def local_image(plan, tables, mask, target, pupil, source_shift, source_weight, halo):
    arrays = {"pupil": pupil, "e_own": tables["e_own"], "e_rim": tables["e_rim"], "halo": halo}
    arrays.update((f"mask{n}", mask) for n in range(0, plan.cols, CHUNK))
    arrays.update((n, tables[n]) for n in ("cols", "up_rows", "up_cols", "weave_rows", "weave_up"))
    arrays["target"] = target
    arrays.update((n, t) for n, t in tables.items() if n not in arrays and n != "own_rows")
    names = tuple(arrays)
    picked = ("e_rim", "final_cols", "final_rows")
    local = {n: a.shape[1:] if n in picked else a.shape for n, a in arrays.items()}
    local.update((n, (TS, CHUNK)) for n in names if n.startswith("mask"))
    distant = pl.BlockSpec(memory_space=pltpu.MemorySpace.HBM)
    sources, group, tile_cols = plan.sources, plan.group, plan.tile_cols
    band, coarse = plan.band, plan.coarse
    return pl.pallas_call(
        functools.partial(image_kernel, plan, names),
        out_shape=[
            jax.ShapeDtypeStruct((2 * band, plan.wide), f32),
            jax.ShapeDtypeStruct((HALO, plan.width), f32),
        ],
        in_specs=[distant] * (2 + len(names)),
        out_specs=[distant] * 2,
        scratch_shapes=[pltpu.VMEM(local[n], arrays[n].dtype) for n in names]
        + [
            pltpu.VMEM((sources, plan.freqs, band), f32),
            pltpu.VMEM((tile_cols, 4, band, band), f32),
            pltpu.VMEM((plan.stores, sources, coarse, 2 * coarse), f32),
            pltpu.VMEM((tile_cols, 2, band, band), f32),
            pltpu.VMEM((2 * band, plan.wide), f32),
            pltpu.VMEM((HALO, plan.width), f32),
            pltpu.VMEM((2 * band, plan.cols), bf16),
            pltpu.VMEM((2 * band, plan.cols), bf16),
            pltpu.VMEM((tile_cols, TS, 2 * coarse), bf16),
            pltpu.VMEM((tile_cols, 2 * band, group * band), bf16),
            pltpu.VMEM((tile_cols, group, coarse, 2 * band), bf16),
            pltpu.SMEM(source_shift.shape[::-1], jnp.int32),
            pltpu.SMEM(source_weight.shape, f32),
            pltpu.SemaphoreType.DMA((len(names) + 2,)),
        ],
        compiler_params=pltpu.CompilerParams(vmem_limit_bytes=60 * 1024 * 1024),
        name="image",
    )(source_shift.T, source_weight, *[jnp.asarray(arrays[n]) for n in names])


def shards(plan, mask, target, pupil, source_shift, source_weight):
    tile_row = lax.axis_index("tile")
    swap = [(0, 1), (1, 0)]
    edge = lax.dynamic_slice_in_dim(mask, jnp.where(tile_row == 0, TS - HALO, 0), HALO, 0)
    halo = lax.ppermute(edge, "tile", swap)
    tables = plan.tables()
    tail, row = local_image(plan, tables, mask, target, pupil, source_shift, source_weight, halo)
    row = lax.ppermute(row, "tile", swap)
    own = own_rows(plan, tables, tail)
    vmem = pl.BlockSpec(memory_space=pltpu.VMEM)
    return pl.pallas_call(
        add_kernel,
        out_shape=jax.ShapeDtypeStruct((TS, plan.width), f32),
        in_specs=[vmem] * 2,
        out_specs=vmem,
        compiler_params=pltpu.CompilerParams(vmem_limit_bytes=8 * 1024 * 1024),
        name="add_rows",
    )(own, row)


def solution(mesh):
    sizes = dict(mesh.shape)

    def run(mask, target, pupil, source_shift, source_weight):
        plan = Plan(pupil.shape[0], mask.shape[1], sizes["src"], source_shift.shape[0])
        placed = (P(("groups", "tile"), None), P(("groups", "tile"), None), P(), P(), P())
        return jax.shard_map(
            functools.partial(shards, plan),
            mesh=mesh,
            in_specs=placed,
            out_specs=P(("groups", "tile"), "src"),
            check_vma=False,
        )(mask, target, pupil, source_shift, source_weight)

    return run
```

```python
import functools
import math

import jax
import jax.numpy as jnp
import ml_dtypes
import numpy as np
from jax import lax
from jax.experimental import pallas as pl
from jax.experimental.pallas import tpu as pltpu
from jax.sharding import PartitionSpec as P

TS = 512
HALO = 64
PAD = TS + 2 * HALO
LANES = 128
FINE = 256
CHUNK = 512
LAG = 1
MOST = 24

resist_gain = 25.0
resist_level = 0.25

f32 = jnp.float32
bf16 = jnp.bfloat16


def halves(table):
    table = np.asarray(table, np.float64)
    high = table.astype(np.float32).astype(ml_dtypes.bfloat16)
    low = (table - high.astype(np.float64)).astype(np.float32).astype(ml_dtypes.bfloat16)
    return high, low


def turns(left, right, period):
    angle = 2.0 * np.pi * np.mod(np.outer(left, right), period) / period
    return np.cos(angle), np.sin(angle)


def both(table, axis):
    return np.concatenate(halves(table), axis=axis)


def split(value):
    high = value.astype(bf16)
    return high, (value - high.astype(f32)).astype(bf16)


def dot(left, right):
    return lax.dot_general(left, right, (((1,), (0,)), ((), ())), preferred_element_type=f32)


class Plan:
    def __init__(self, freqs, cols, n_src, sources):
        self.freqs = freqs
        self.reach = (3 * freqs) // 8
        self.band = 2 * freqs
        self.coarse = 2 * freqs
        self.cols = cols
        self.tile_cols = cols // TS
        self.width = cols // n_src
        self.wide = -(-self.width // LANES) * LANES
        self.n_src = n_src
        self.sources = sources
        self.group = max(n for n in range(2, MOST + 1, 2) if sources % n == 0)
        self.stores = self.tile_cols if sources <= MOST else 1
        self.spans = [
            (max(0, c * TS - LANES), min(cols, (c + 1) * TS + LANES)) for c in range(self.tile_cols)
        ]

    def tables(self):
        freqs, band, coarse = self.freqs, self.band, self.coarse
        index = np.arange(band)
        used = (index < freqs + 2 * self.reach).astype(np.float64)
        centre = index - (freqs // 2 + self.reach)
        out = {}
        cosine, sine = turns(centre, np.arange(PAD), PAD)
        rows = np.concatenate([cosine, -sine], axis=0) * np.concatenate([used, used])[:, None]
        out["e_own"] = both(rows[:, HALO : HALO + TS], 0)
        rims = []
        for rim in (rows[:, HALO + TS :], rows[:, :HALO]):
            high, low = halves(rim)
            rims.append(np.concatenate([high, low, high], axis=1))
        out["e_rim"] = np.stack(rims)

        def fold(real, imag):
            return np.concatenate(
                [real[:, :freqs], imag[:, :freqs], real[:, freqs:], imag[:, freqs:]], axis=1
            )

        place = np.arange(-LANES, TS + LANES) + HALO
        inside = ((place >= 0) & (place < PAD)).astype(np.float64)[:, None] * used
        cosine, sine = turns(place, centre, PAD)
        out["cols"] = both(fold(cosine * inside, -sine * inside), 1)
        relative = np.arange(freqs) - freqs // 2
        points = np.arange(coarse)
        cosine, sine = turns(points, relative, coarse)
        high, low = halves(np.concatenate([cosine, -sine], axis=1))
        out["up_rows"] = np.concatenate(
            [np.concatenate([high, high], axis=1), np.concatenate([low, low], axis=1)], axis=0
        )
        high, low = halves(np.concatenate([cosine.T, sine.T], axis=0))
        out["down_rows"] = np.concatenate(
            [np.concatenate([high, high], axis=1), np.concatenate([low, low], axis=1)], axis=0
        )
        order = np.concatenate([points[::2], points[1::2]])
        up, down = [], []
        for some in (points[::2], points[1::2]):
            cosine, sine = turns(centre[:freqs], some, coarse)
            table = np.concatenate(
                [np.concatenate([cosine, sine], axis=1), np.concatenate([-sine, cosine], axis=1)], axis=0
            )
            for into, piece in ((up, table), (down, table.T)):
                pair = both(piece, 1)
                into.append(np.concatenate([pair, pair], axis=0))
        out["up_cols"], out["down_cols"] = np.stack(up), np.stack(down)
        spread = (np.arange(TS) + HALO)[:, None] - (PAD // coarse) * points[None, :]
        weave = np.ones(spread.shape)
        for p in range(1, freqs):
            weave = weave + 2.0 * np.cos(2.0 * np.pi * np.mod(p * spread, PAD) / PAD)
        weave = weave / coarse
        out["weave_rows"] = both(weave, 1)
        out["weave_cols"] = both(weave[:, order], 1)
        turned = both(weave[:, order].T, 1)
        out["weave_up"] = np.concatenate([turned, turned], axis=0)
        out["weave_down"] = both(weave.T, 0)
        blocks = []
        for j in range(self.n_src):
            pieces = []
            for c in range(self.tile_cols):
                place = np.arange(j * self.width, (j + 1) * self.width) - c * TS + HALO
                inside = ((place >= 0) & (place < PAD)).astype(np.float64)[:, None] * used
                cosine = np.zeros((self.wide, band))
                sine = np.zeros((self.wide, band))
                cosine[: self.width], sine[: self.width] = turns(place, centre, PAD)
                cosine[: self.width] *= inside
                sine[: self.width] *= inside
                pieces.append(
                    np.concatenate([fold(cosine, -sine), fold(sine, cosine)], axis=0).T
                )
            blocks.append(both(np.concatenate(pieces, axis=0), 1))
        out["final_cols"] = np.stack(blocks)
        out["own_rows"] = np.stack(halves(rows.T[HALO : HALO + TS]))
        out["final_rows"] = np.stack([both(rows.T[HALO + TS :], 0), both(rows.T[:HALO], 0)])
        return {name: np.ascontiguousarray(value) for name, value in out.items()}


def merged(*lists):
    keyed = [((i + 0.5) / len(steps), n, step) for n, steps in enumerate(lists) for i, step in enumerate(steps)]
    return [step for _, _, step in sorted(keyed, key=lambda item: item[:2])]


def run(steps):
    for step in steps:
        step()


def image_kernel(plan, names, shift_far, weight_far, *refs):
    far = dict(zip(names, refs[: len(names)]))
    tail_out, row_out = refs[len(names) : len(names) + 2]
    near = dict(zip(names, refs[len(names) + 2 :]))
    (
        pupils, spectrum, fields, grads, tail, rim, u_high, u_low, woven, lifts, lines, shift, weight, sems,
    ) = refs[2 * len(names) + 2 :]
    sources, group = plan.sources, plan.group
    freqs, reach, band, coarse = plan.freqs, plan.reach, plan.band, plan.coarse
    tile_row = lax.axis_index("tile")
    block = lax.axis_index("src")
    picked = {"e_rim": tile_row, "final_cols": block, "final_rows": tile_row}
    scalars = [
        pltpu.make_async_copy(shift_far, shift, sems.at[len(names)]),
        pltpu.make_async_copy(weight_far, weight, sems.at[len(names) + 1]),
    ]
    for copy in scalars:
        copy.start()
    pending = {}
    spans = {f"mask{n}": slice(n, n + CHUNK) for n in range(0, plan.cols, CHUNK)}
    for i, name in enumerate(names):
        source = far[name].at[picked[name]] if name in picked else far[name]
        if name in spans:
            source = source.at[:, spans[name]]
        pending[name] = pltpu.make_async_copy(source, near[name], sems.at[i])
    early = [name for name in names if name in ("pupil", "e_own", "e_rim", "halo", "cols") or name in spans]
    for name in early:
        pending[name].start()

    def need(*wanted):
        for name in wanted:
            if name in pending:
                pending.pop(name).wait()

    tabs = near
    target_v, e_rim, final_tab, halo = (
        near[name] for name in ("target", "e_rim", "final_cols", "halo")
    )
    for copy in scalars:
        copy.wait()
    total = weight[0]
    for s in range(1, sources):
        total = total + weight[s]
    scale = 1.0 / (PAD * PAD)
    lane = lax.broadcasted_iota(jnp.int32, (1, band), 1)
    first_half = lane < freqs
    residue = jnp.where(first_half, lane, lane - freqs)
    sign = jnp.where(first_half, 1.0, -1.0).astype(f32)
    need("pupil")
    doubled = jnp.concatenate([near["pupil"][...]] * 2, axis=1)

    def place_pupil(s):
        strength = jnp.sqrt(jnp.full((1, band), weight[s] / total, f32)) * scale
        pupils[s] = pltpu.roll(doubled, shift[1, s] + reach, 1) * strength

    if sources <= MOST:
        for s in range(sources):
            place_pupil(s)
    else:
        lax.fori_loop(0, sources, lambda s, c: (place_pupil(s), c)[1], 0)

    need("e_own", "e_rim", "halo")
    for name, cols in spans.items():
        need(name)
        if cols.start == 0:
            for late in names:
                if late not in early:
                    pending[late].start()
        rim_high, rim_low = split(halo[:, cols])
        rows = dot(e_rim[...], jnp.concatenate([rim_high, rim_high, rim_low], axis=0))
        high, low = split(near[name][...])
        part = dot(near["e_own"][...], high)
        rows = rows + part[: 2 * band] + part[2 * band :] + dot(near["e_own"][: 2 * band, :], low)
        high, low = split(rows)
        u_high[:, cols] = high
        u_low[:, cols] = low
    need("cols")

    def transform(c):
        first, last = plan.spans[c]
        inside = slice(first - c * TS + LANES, last - c * TS + LANES)
        prod = dot(u_high[:, first:last], tabs["cols"][inside, :])
        prod = prod[:, : 2 * band] + prod[:, 2 * band :]
        prod = prod + dot(u_low[:, first:last], tabs["cols"][inside, : 2 * band])
        for k in range(2):
            own, other = prod[:band, k * band : (k + 1) * band], prod[band:, k * band : (k + 1) * band]
            half = own - sign * pltpu.roll(other, freqs, 1)
            spectrum[c, k] = half
            spectrum[c, 2 + k] = pltpu.roll(half, freqs, 1) * sign

    def lane_block(value, k):
        return value[:, k * band : (k + 1) * band]

    pairs = group // 2
    state = {}

    def gather(c, first, i):
        for k in (2 * i, 2 * i + 1):
            down = shift[0, first + k] + reach
            along = shift[1, first + k] + reach
            rows = pl.ds(down, freqs)
            close = residue >= along
            upper = jnp.where(close, spectrum[c, 0, rows, :], spectrum[c, 1, rows, :])
            lower = jnp.where(close, spectrum[c, 2, rows, :], spectrum[c, 3, rows, :])
            scaled = pupils[first + k]
            high, low = split(jnp.concatenate([upper * scaled, lower * scaled], axis=0))
            lifts[c, :band, k * band : (k + 1) * band] = high
            lifts[c, band:, k * band : (k + 1) * band] = low

    def lift(c, first, i):
        lifted = dot(tabs["up_rows"][...], lifts[c, :, 2 * i * band : 2 * (i + 1) * band])
        high, low = split(lifted[:coarse] + lifted[coarse:])
        for k in range(2):
            lines[c, 2 * i + k, :, :band] = lane_block(high, k)
            lines[c, 2 * i + k, :, band:] = lane_block(low, k)

    def light_up(c, first, i):
        for k in (2 * i, 2 * i + 1):
            along = shift[1, first + k] + reach
            flip = jnp.where(residue >= along, 1.0, -1.0).astype(bf16)
            line = lines[c, k]
            even = dot(line, tabs["up_cols"][0])
            odd = dot(line * jnp.concatenate([flip, flip], axis=1), tabs["up_cols"][1])
            field = jnp.concatenate(
                [even[:, :coarse] + even[:, coarse:], odd[:, :coarse] + odd[:, coarse:]], axis=1
            )
            fields[c % plan.stores, first + k] = field
            state["power", c] = state["power", c] + field * field

    def fine_steps(c):
        def begin():
            power = state.pop(("power", c))
            even, odd = power[:, :coarse], power[:, coarse:]
            power = jnp.where(first_half, even + pltpu.roll(even, freqs, 1), odd + pltpu.roll(odd, freqs, 1))
            high, low = split(power)
            pair = jnp.concatenate([high, low], axis=1)
            state["quad", c] = jnp.concatenate([pair, pair], axis=0)

        def rows_of(m):
            return slice(m * FINE, (m + 1) * FINE)

        def weave_rows(m):
            left = dot(tabs["weave_rows"][rows_of(m), :], state["quad", c])
            high, low = split(left[:, :coarse] + left[:, coarse:])
            state["a", c, m] = jnp.concatenate([high, low], axis=1)

        def slope_rows(m):
            light = dot(state.pop(("a", c, m)), tabs["weave_up"][...])
            light = light[:, :TS] + light[:, TS:]
            bend = jnp.tanh((0.5 * resist_gain) * light - 0.5 * resist_gain * resist_level)
            wanted = target_v[rows_of(m), c * TS : (c + 1) * TS]
            slope = ((0.25 * resist_gain) * (bend + 1.0) - (0.5 * resist_gain) * wanted) * (1.0 - bend * bend)
            state["g", c, m] = split(slope)

        def fold_rows(m):
            high, low = state.pop(("g", c, m))
            part = dot(high, tabs["weave_cols"][...]) + dot(low, tabs["weave_cols"][...])
            high, low = split(part[:, :coarse] + part[:, coarse:])
            woven[c, rows_of(m), :] = jnp.concatenate([high, low], axis=1)

        def finish():
            part = dot(tabs["weave_down"][...], woven[c])
            part = part[:coarse] + part[coarse:]
            pull = 2.0 * (part[:, :coarse] + part[:, coarse:])
            turned = pltpu.roll(pull, freqs, 1)
            state["pull", c] = jnp.concatenate(
                [jnp.where(first_half, pull, turned), jnp.where(first_half, turned, pull)], axis=1
            )

        stages = (weave_rows, slope_rows, fold_rows)
        count = TS // FINE
        middle = [
            functools.partial(stages[k], t - k)
            for t in range(count + 2) for k in (2, 1, 0) if 0 <= t - k < count
        ]
        return [begin] + middle + [finish]

    def fall(c, first, i):
        for k in (2 * i, 2 * i + 1):
            high, low = split(fields[c % plan.stores, first + k] * state["pull", c])
            sums = []
            for h in range(2):
                left = jnp.concatenate([lane_block(high, h), lane_block(low, h)], axis=1)
                part = dot(left, tabs["down_cols"][h])
                sums.append(part[:, :band] + part[:, band:])
            along = shift[1, first + k] + reach
            flip = jnp.where(residue >= along, 1.0, -1.0).astype(f32)
            high, low = split(sums[0] + flip * sums[1])
            lifts[c, :band, k * band : (k + 1) * band] = high
            lifts[c, band:, k * band : (k + 1) * band] = low

    def settle(c, first, i):
        part = dot(tabs["down_rows"][...], lifts[c, :, 2 * i * band : 2 * (i + 1) * band])
        part = part[:band] + part[band:]
        for k in range(2):
            s = first + 2 * i + k
            mine = lane_block(part, k)
            mine = (mine[:freqs] + sign * pltpu.roll(mine[freqs:], freqs, 1)) * pupils[s]
            rows = pl.ds(shift[0, s] + reach, freqs)
            close = residue >= shift[1, s] + reach
            zero = jnp.zeros_like(mine)
            grads[c, 0, rows, :] += jnp.where(close, mine, zero)
            grads[c, 1, rows, :] += jnp.where(close, zero, mine)

    def steps(stage, c, first=0):
        return [functools.partial(stage, c, first, i) for i in range(pairs)]

    grads[...] = jnp.zeros_like(grads)
    tiles = range(plan.tile_cols)
    rounds = sources // group
    if rounds == 1:
        for c in tiles:
            state["power", c] = jnp.zeros((coarse, 2 * coarse), f32)
        stages = [
            lambda c: [functools.partial(transform, c)],
            lambda c: steps(gather, c),
            lambda c: steps(lift, c),
            lambda c: steps(light_up, c),
            fine_steps,
            lambda c: steps(fall, c),
            lambda c: steps(settle, c),
        ]
        wants = {
            2: ("up_rows", "up_cols"),
            4: ("target", "weave_rows", "weave_up", "weave_cols", "weave_down"),
            5: ("down_rows", "down_cols"),
        }
        slots = []
        for t in range(len(stages) + LAG * (plan.tile_cols - 1)):
            slots.append([stages[t - LAG * c](c) for c in tiles if 0 <= t - LAG * c < len(stages)])
        falls, settles, half = slots[-2].pop(), slots.pop()[0], (pairs + 1) // 2
        slots[-1].append(falls[:half])
        slots += [[falls[half:], settles[:half]], [settles[half:]]]
        for t, slot in enumerate(slots):
            need(*wants.get(t, ()))
            run(merged(*slot))
    else:
        need(*(name for name in names if not name.startswith("final")))
        for c in tiles:
            transform(c)

            def forward(g, power):
                state["power", c] = power
                for stage in (gather, lift, light_up):
                    run(steps(stage, c, g * group))
                return state["power", c]

            def backward(g, carry):
                for stage in (fall, settle):
                    run(steps(stage, c, g * group))
                return carry

            state["power", c] = lax.fori_loop(0, rounds, forward, jnp.zeros((coarse, 2 * coarse), f32))
            run(fine_steps(c))
            lax.fori_loop(0, rounds, backward, 0)

    need("final_cols", "final_rows")
    wide = plan.wide
    bands = jnp.concatenate([grads[c, k] for c in range(plan.tile_cols) for k in range(2)], axis=1)
    high, low = split(bands)
    part = dot(high, final_tab[...])
    part = part[:, : 2 * wide] + part[:, 2 * wide :] + dot(low, final_tab[:, : 2 * wide])
    column_part = jnp.concatenate([part[:, :wide], part[:, wide:]], axis=0)
    tail[...] = column_part
    ends = [pltpu.make_async_copy(tail, tail_out, sems.at[0]), pltpu.make_async_copy(rim, row_out, sems.at[1])]
    ends[0].start()
    high, low = split(column_part)
    table = near["final_rows"]
    part = dot(table[...], high)
    part = part[:HALO] + part[HALO:] + dot(table[:HALO, :], low)
    rim[...] = part[:, : plan.width]
    ends[1].start()
    for end in ends:
        end.wait()


def own_kernel(plan, tail, table, out):
    high, low = split(tail[...])
    part = dot(table[0], high) + dot(table[0], low) + dot(table[1], high)
    out[...] = part[:, : plan.width]


def add_kernel(own, row, out):
    tile_row = lax.axis_index("tile")
    out[...] = own[...]
    first = pl.multiple_of(jnp.where(tile_row == 0, TS - HALO, 0), HALO)
    out[pl.ds(first, HALO), :] = own[pl.ds(first, HALO), :] + row[...]


def own_rows(plan, tables, tail):
    vmem = pl.BlockSpec(memory_space=pltpu.VMEM)
    return pl.pallas_call(
        functools.partial(own_kernel, plan),
        out_shape=jax.ShapeDtypeStruct((TS, plan.width), f32),
        in_specs=[vmem] * 2,
        out_specs=vmem,
        compiler_params=pltpu.CompilerParams(vmem_limit_bytes=8 * 1024 * 1024),
        cost_estimate=pl.CostEstimate(flops=10**9, bytes_accessed=10**6, transcendentals=0),
        name="own_rows",
    )(tail, jnp.asarray(tables["own_rows"]))


def local_image(plan, tables, mask, target, pupil, source_shift, source_weight, halo):
    arrays = {"pupil": pupil, "e_own": tables["e_own"], "e_rim": tables["e_rim"], "halo": halo}
    arrays.update((f"mask{n}", mask) for n in range(0, plan.cols, CHUNK))
    arrays.update((n, tables[n]) for n in ("cols", "up_rows", "up_cols", "weave_rows", "weave_up"))
    arrays["target"] = target
    arrays.update((n, t) for n, t in tables.items() if n not in arrays and n != "own_rows")
    names = tuple(arrays)
    picked = ("e_rim", "final_cols", "final_rows")
    local = {n: a.shape[1:] if n in picked else a.shape for n, a in arrays.items()}
    local.update((n, (TS, CHUNK)) for n in names if n.startswith("mask"))
    distant = pl.BlockSpec(memory_space=pltpu.MemorySpace.HBM)
    sources, group, tile_cols = plan.sources, plan.group, plan.tile_cols
    band, coarse = plan.band, plan.coarse
    return pl.pallas_call(
        functools.partial(image_kernel, plan, names),
        out_shape=[
            jax.ShapeDtypeStruct((2 * band, plan.wide), f32),
            jax.ShapeDtypeStruct((HALO, plan.width), f32),
        ],
        in_specs=[distant] * (2 + len(names)),
        out_specs=[distant] * 2,
        scratch_shapes=[pltpu.VMEM(local[n], arrays[n].dtype) for n in names]
        + [
            pltpu.VMEM((sources, plan.freqs, band), f32),
            pltpu.VMEM((tile_cols, 4, band, band), f32),
            pltpu.VMEM((plan.stores, sources, coarse, 2 * coarse), f32),
            pltpu.VMEM((tile_cols, 2, band, band), f32),
            pltpu.VMEM((2 * band, plan.wide), f32),
            pltpu.VMEM((HALO, plan.width), f32),
            pltpu.VMEM((2 * band, plan.cols), bf16),
            pltpu.VMEM((2 * band, plan.cols), bf16),
            pltpu.VMEM((tile_cols, TS, 2 * coarse), bf16),
            pltpu.VMEM((tile_cols, 2 * band, group * band), bf16),
            pltpu.VMEM((tile_cols, group, coarse, 2 * band), bf16),
            pltpu.SMEM(source_shift.shape[::-1], jnp.int32),
            pltpu.SMEM(source_weight.shape, f32),
            pltpu.SemaphoreType.DMA((len(names) + 2,)),
        ],
        compiler_params=pltpu.CompilerParams(vmem_limit_bytes=60 * 1024 * 1024),
        name="image",
    )(source_shift.T, source_weight, *[jnp.asarray(arrays[n]) for n in names])


def shards(plan, mask, target, pupil, source_shift, source_weight):
    tile_row = lax.axis_index("tile")
    swap = [(0, 1), (1, 0)]
    edge = lax.dynamic_slice_in_dim(mask, jnp.where(tile_row == 0, TS - HALO, 0), HALO, 0)
    halo = lax.ppermute(edge, "tile", swap)
    tables = plan.tables()
    tail, row = local_image(plan, tables, mask, target, pupil, source_shift, source_weight, halo)
    row = lax.ppermute(row, "tile", swap)
    own = own_rows(plan, tables, tail)
    vmem = pl.BlockSpec(memory_space=pltpu.VMEM)
    return pl.pallas_call(
        add_kernel,
        out_shape=jax.ShapeDtypeStruct((TS, plan.width), f32),
        in_specs=[vmem] * 2,
        out_specs=vmem,
        compiler_params=pltpu.CompilerParams(vmem_limit_bytes=8 * 1024 * 1024),
        name="add_rows",
    )(own, row)


def solution(mesh):
    sizes = dict(mesh.shape)

    def run(mask, target, pupil, source_shift, source_weight):
        plan = Plan(pupil.shape[0], mask.shape[1], sizes["src"], source_shift.shape[0])
        placed = (P(("groups", "tile"), None), P(("groups", "tile"), None), P(), P(), P())
        return jax.shard_map(
            functools.partial(shards, plan),
            mesh=mesh,
            in_specs=placed,
            out_specs=P(("groups", "tile"), "src"),
            check_vma=False,
        )(mask, target, pupil, source_shift, source_weight)

    return run
```
